256 devices in a mesh: group: 8 (over x, core), shard: 32 (over y, z).
Axes of the slice: x: 4, y: 4, z: 8, core: 2. Of those that a mesh axis runs over, the one named last changes fastest.
Arguments:
- caption_embed: bfloat16 [1024, 256], P(('group', 'shard')), may hold values from -12 to 12
- gallery_embed: bfloat16 [131072, 256], P('shard'), may hold values from -6 to 6
- probe_blocks: int32 [8, 128], P('group'), may hold values from 0 to 511, all different within a row
- query_states: bfloat16 [1024, 32, 768], P(('group', 'shard')), may hold values from -136 to 136
- patches: bfloat16 [32, 257, 1408], P('shard'), may hold values from -6 to 6
- candidates: int32 [1024, 16, 1], P(('group', 'shard')), may hold values from 0 to 31; in each aligned block of 64 rows (0 to 63, 64 to 127, ..., all dimensions but the last counted through in order) at most 3 rows name the same one
- query_weight: bfloat16 [768, 768], replicated, may hold values from -0.21875 to 0.21875
- keyvalue_weight: bfloat16 [1408, 1536], P(None, 'group'), may hold values from -0.15625 to 0.15625
- output_weight: bfloat16 [768, 768], replicated, may hold values from -0.21875 to 0.21875
- norm_gain: float32 [768], replicated, may hold values from 0.5 to 1.5
- norm_bias: float32 [768], replicated, may hold values from -3 to 3
Outputs:
- layer_out: bfloat16 [1024, 16, 32, 768], P(('group', 'shard'))
- normalizer: float32 [1024], P(('group', 'shard'))
The draws below stay inside these ranges and needn't reach their ends.
Inputs may be any that keep to these rules, and one draw needn't show every extreme that they name: `candidates`: within the 64 candidate entries of the captions of one device, no image id occurs more than 3 times; a caption may name an image twice. `probe_blocks`: the 128 ids of one group are distinct.
All inputs are finite; a program needn't handle non-finite values.
Results may differ from the reference program's by a relative error of at most 0.0025.
The reference program's roundings to bfloat16 on the way count: a program that leaves them out, or rounds other values in their place, can miss the bound.
Values may be sent and summed in bfloat16 or wider, within the bound.
No kernel may reach another device: no remote copies, remote signals or barrier semaphores. Data moves between devices by JAX's collectives and lax.ppermute only.
A program may use at most 128 MiB of HBM per device.

```python
import math
import jax
import jax.numpy as jnp
import numpy as np
from jax import lax

EMB = 256
DQ = 768
DV = 1408
HEADS = 12
HD = 64
NQ = 32
NP = 257
CAND = 16
BLK = 256
CAP_DEV = 4
CAP_GRP = 128
CAPTIONS = 1024
N_IMG = 32
NB_ALL = 512
PROBE = 128
SLOT = 3
N_GROUP = 8


def draw_caption_embed(key, part):
    key = jax.random.fold_in(key, 11)
    base_key = jax.random.fold_in(key, 0)
    base_values = jnp.clip(jax.random.normal(base_key, (CAPTIONS, EMB), jnp.float32), -4.0, 4.0)
    return base_values.astype(jnp.bfloat16)


def draw_query_states(key, part):
    key = jax.random.fold_in(key, 23)
    base_key = jax.random.fold_in(key, 0)
    base_values = jnp.clip(jax.random.normal(base_key, (CAPTIONS, NQ, DQ), jnp.float32), -4.0, 4.0)
    return base_values.astype(jnp.bfloat16)


def block_scale(key, shape, shards, low, largest):
    loudness, own = 1.0, jax.random.fold_in(key, 6)
    for axis_at, parts in shards:
        draws = jnp.exp(jax.random.uniform(jax.random.fold_in(own, axis_at), (parts,), jnp.float32, low / len(shards), largest / len(shards)))
        loudness = loudness * jnp.repeat(draws, shape[axis_at] // parts).reshape([-1 if axis == axis_at else 1 for axis in range(len(shape))])
    return loudness


def different_ones(stream_key, rows, amount, top, lift):
    order = jax.random.permutation(jax.random.fold_in(stream_key, 1), amount)
    favour = order
    for power in range(3):
        favour = favour * favour // amount
    favour = favour * lift // amount
    chance = jax.random.randint(jax.random.fold_in(stream_key, 2), (rows, amount), 0, 4096) + favour
    holders = jax.random.permutation(jax.random.fold_in(stream_key, 3), rows)[jnp.arange(amount) % rows]
    chance = jnp.where(jnp.arange(rows)[:, None] == holders[None, :], 1 << 14, chance)
    priority = chance * amount + jnp.arange(amount)
    return lax.top_k(priority.astype(jnp.int32), top)[1].astype(jnp.int32)


def assign_block(own_key, own, number, rows, number_of, top, limit, lean):
    order = jax.random.permutation(own_key, number_of)
    packed, common = shares(number_of, rows * top, limit, lean, True), shares(number_of, rows * top, limit, lean, False)
    places = jnp.arange(number_of)

    def named(lengths, offset_by):
        used = int((lengths > 0).sum())
        fixed = max(1, used // 4)
        passed = fixed + (places - fixed + offset_by * (used - fixed)) % max(1, number_of - fixed)
        return jnp.zeros((number_of,), jnp.int32).at[order[jnp.where(places < fixed, places, passed)]].set(jnp.asarray(lengths, jnp.int32))

    lengths = jnp.where(number % 4 == 0, named(packed, number // 4), named(common, number - number // 4 - 1))
    mixed = jax.random.permutation(jax.random.fold_in(own, 3), number_of)
    donor, taker = mixed[0:number_of // 2 * 2:2], mixed[1:number_of // 2 * 2:2]
    room = jnp.minimum(lengths[donor] - 1, limit - lengths[taker]) // 2
    room = jnp.where((donor == order[0]) | (taker == order[0]) | (lengths[taker] == 0), 0, jnp.maximum(room, 0))
    passed = jax.random.randint(jax.random.fold_in(own, 4), (number_of // 2,), 0, 1 << 20) % (room + 1)
    lengths = lengths.at[donor].add(-passed).at[taker].add(passed)
    labels = jnp.searchsorted(jnp.cumsum(lengths), jnp.arange(rows * top), side="right").astype(jnp.int32)
    grid = labels.reshape(top, rows).T
    grid = grid[jax.random.permutation(jax.random.fold_in(own, 1), rows)]
    offset_by = jax.random.randint(jax.random.fold_in(own, 2), (rows, 1), 0, top)
    return jnp.take_along_axis(grid, (jnp.arange(top)[None, :] + offset_by) % top, axis=1)


def shares(count, total, bound, skew, full):
    portions = [(1 << 20) // math.isqrt(grade ** skew) + 1 for grade in range(1, count + 1)]
    largest = bound if full else min(bound, max(-(-total // count), total * portions[0] // sum(portions)))
    least = 1 if total - largest >= count - 1 else 0
    holding, spare = [largest] + [least] * (count - 1), total - largest - least * (count - 1)
    while spare > 0:
        free = [i for i in range(1, count) if holding[i] < largest] or [i for i in range(1, count) if holding[i] < bound]
        mass, remaining = sum([portions[i] for i in free]), spare
        for i in free:
            extra = min(bound - holding[i], max(1, remaining * portions[i] // mass), spare)
            holding[i] = holding[i] + extra
            spare = spare - extra
    return np.array(holding)


def bell_draw(own_key, shape, spread, reach, cuts=(), dtype=jnp.bfloat16):
    drawn = jax.random.normal(own_key, shape, jnp.float32) * spread
    if len(cuts) > 0:
        drawn = block_scale(own_key, shape, cuts, -0.22, 0.18) * drawn
    return jnp.clip(drawn, min=-reach, max=reach).astype(dtype)


def setup_inputs(seed: int = 0) -> dict:
    streams_of = jax.random.split(jax.random.key(seed), 12)
    caption_embed = draw_caption_embed(jax.random.fold_in(streams_of[11], 71), 0)
    gallery_embed = bell_draw(streams_of[1], (NB_ALL * BLK, EMB), 1.0, 6.0, ((0, 32),))
    probe_blocks = different_ones(streams_of[2], N_GROUP, NB_ALL, PROBE, 4096)
    query_states = draw_query_states(jax.random.fold_in(streams_of[11], 71), 0)
    patches = bell_draw(streams_of[4], (N_IMG, NP, DV), 1.0, 6.0, ((0, 32),))
    candidates_keys = jax.random.split(jax.random.fold_in(streams_of[5], 1), CAPTIONS * CAND // (CAP_DEV * CAND))
    candidates_turns = jax.random.permutation(jax.random.fold_in(streams_of[5], 3), CAPTIONS * CAND // (CAP_DEV * CAND))
    candidates = jax.vmap(lambda own, number: assign_block(jax.random.fold_in(streams_of[5], 2), own, number, CAP_DEV * CAND, N_IMG, 1, SLOT, 2))(candidates_keys, candidates_turns).reshape((CAPTIONS, CAND, 1))
    query_weight = bell_draw(streams_of[6], (DQ, DQ), DQ ** -0.5, 0.21875)
    keyvalue_weight = bell_draw(streams_of[7], (DV, 2 * DQ), DV ** -0.5, 0.15625, ((1, 8),))
    output_weight = bell_draw(streams_of[8], (DQ, DQ), DQ ** -0.5, 0.21875)
    norm_gain = jnp.clip(1.0 + 0.1 * jax.random.normal(streams_of[9], (DQ,), jnp.float32), 0.5, 1.5)
    norm_bias = bell_draw(streams_of[10], (DQ,), 0.5, 3.0, (), jnp.float32)
    return {"caption_embed": caption_embed, "gallery_embed": gallery_embed, "probe_blocks": probe_blocks, "query_states": query_states, "patches": patches, "candidates": candidates, "query_weight": query_weight, "keyvalue_weight": keyvalue_weight, "output_weight": output_weight, "norm_gain": norm_gain, "norm_bias": norm_bias}


def layer_norm(hidden, gain_row, bias_row):
    average = lax.optimization_barrier(jnp.mean(hidden, axis=-1, keepdims=True))
    centered = hidden - average
    variance = lax.optimization_barrier(jnp.mean(centered * centered, axis=-1, keepdims=True))
    return centered * lax.rsqrt(variance + 1e-06) * gain_row + bias_row

def reference(caption_embed, gallery_embed, probe_blocks, query_states, patches, candidates, query_weight, keyvalue_weight, output_weight, norm_gain, norm_bias):
    sim_scale = 1.0 / (0.07 * math.sqrt(EMB))
    blocks = gallery_embed.reshape(NB_ALL, BLK, EMB)
    group_captions = caption_embed.reshape(N_GROUP, CAP_GRP, EMB)

    def group_normalizer(inputs):
        caption_rows, block_ids = inputs
        probed = blocks[block_ids].reshape(PROBE * BLK, EMB)
        scores = jnp.dot(caption_rows, probed.T, preferred_element_type=jnp.float32) * sim_scale
        return jax.nn.logsumexp(scores, axis=-1)
    normalizer = lax.map(group_normalizer, (group_captions, probe_blocks)).reshape(CAPTIONS)
    queries = jnp.dot(query_states.reshape(-1, DQ), query_weight, preferred_element_type=jnp.float32)
    queries = queries.astype(jnp.bfloat16).reshape(CAPTIONS, NQ, DQ)
    keyvalue = jnp.dot(patches.reshape(-1, DV), keyvalue_weight, preferred_element_type=jnp.float32)
    keyvalue = keyvalue.astype(jnp.bfloat16).reshape(N_IMG, NP, 2, HEADS, HD)
    inverse_root = 1.0 / math.sqrt(HD)

    def one_caption(inputs):
        query_rows, states, image_ids = inputs
        chosen = keyvalue[image_ids[:, 0]]
        key_rows = chosen[:, :, 0].astype(jnp.float32)
        value_rows = chosen[:, :, 1].astype(jnp.float32)
        query_heads = query_rows.reshape(NQ, HEADS, HD).astype(jnp.float32)
        scores = jnp.einsum('qhd,cphd->chqp', query_heads, key_rows) * inverse_root
        softmax_rows = jax.nn.softmax(scores, axis=-1).astype(jnp.bfloat16)
        softmax_rows = lax.optimization_barrier(softmax_rows).astype(jnp.float32)
        context = jnp.einsum('chqp,cphd->cqhd', softmax_rows, value_rows).astype(jnp.bfloat16)
        context = context.reshape(CAND * NQ, DQ)
        mixed_rows = jnp.dot(context, output_weight, preferred_element_type=jnp.float32).reshape(CAND, NQ, DQ)
        mixed_rows = mixed_rows + states.astype(jnp.float32)[None]
        return layer_norm(mixed_rows, norm_gain, norm_bias).astype(jnp.bfloat16)
    layer_out = lax.map(one_caption, (queries, query_states, candidates))
    return (layer_out, normalizer)
```

```python
import functools
import math

import jax
import jax.numpy as jnp
from jax import lax
from jax.experimental import pallas as pl
from jax.experimental.pallas import tpu as pltpu
from jax.sharding import PartitionSpec as P

HEADS = 12
BLK = 256
HD = 64
NQ = 32
SLOTS = 12
HROWS = 144
BROWS = 3 * HROWS
EXP_SCALE = math.log2(math.e) / math.sqrt(HD)
F32 = jnp.float32
BF16 = jnp.bfloat16


def project_kernel(group_ref, patches_ref, weight_ref, out_ref):
    kv = jnp.dot(patches_ref[0], weight_ref[...], preferred_element_type=F32)
    last = kv[256:257].astype(BF16)
    body = kv[:256]
    out_ref[...] = jnp.zeros_like(out_ref)
    for h in range(3):
        out_ref[h * HROWS + 128 : h * HROWS + 129, 0:HD] = last[:, h * HD : (h + 1) * HD]

    @pl.when(group_ref[0] < 4)
    def _():
        for h in range(3):
            out_ref[h * HROWS : h * HROWS + 128, 0:HD] = body[:128, h * HD : (h + 1) * HD].astype(BF16)
            out_ref[h * HROWS : h * HROWS + 128, HD:128] = body[128:, h * HD : (h + 1) * HD].astype(BF16)

    @pl.when(group_ref[0] >= 4)
    def _():
        turned = body.T
        for h in range(3):
            rows = turned[h * HD : (h + 1) * HD].astype(BF16)
            out_ref[h * HROWS : h * HROWS + HD] = rows[:, :128]
            out_ref[h * HROWS + HD : h * HROWS + 128] = rows[:, 128:]


def attend_kernel(
    core_ref,
    image_ref,
    count_ref,
    table_ref,
    q0,
    q1,
    q2,
    q3,
    *refs,
):
    own_refs, other_refs = refs[0:4], refs[4:8]
    out_refs = refs[8:12]
    query, held, result, sems = refs[12:16]
    step = pl.program_id(0)

    @pl.when(step == 0)
    def _():
        left = lax.broadcasted_iota(jnp.int32, (128, 128), 1) < HD
        for d, q_ref in enumerate((q0, q1, q2, q3)):
            rows = q_ref[0:128, :].astype(F32)
            first, second = rows[:, 0:128], rows[:, 128:256]
            turned = pltpu.roll(first, HD, 1)
            parts = (
                (jnp.where(left, first, 0.0), jnp.where(left, 0.0, turned)),
                (jnp.where(left, turned, 0.0), jnp.where(left, 0.0, first)),
                (second, pltpu.roll(second, HD, 1)),
            )
            for h in range(3):
                for side in range(2):
                    for c in range(4):
                        query[h, side, d * 4 + c] = parts[h][side][c * 32 : (c + 1) * 32].astype(BF16)

    first_core = core_ref[0] == 0
    for r in range(4):

        @pl.when(step // 8 == r)
        def _():
            mine, theirs = own_refs[r][0], other_refs[r][0]
            held[0] = jnp.where(first_core, mine, theirs)
            held[1] = jnp.where(first_core, theirs, mine)

    image = image_ref[step]
    count = count_ref[image]
    columns = []
    for h in range(3):
        block = held[1, h * HROWS + 128 : (h + 1) * HROWS, :].astype(F32)
        columns.append(block.T[0:HD, 0:1])

    def tile(t, carry):
        pairs = [table_ref[image * SLOTS + jnp.minimum(t * 4 + j, count - 1)] for j in range(4)]
        caps = [lax.shift_right_logical(p, 4) for p in pairs]
        contexts = []
        for h in range(3):
            q = jnp.concatenate(
                [query[h, 0, c] for c in caps] + [query[h, 1, c] for c in caps], axis=0
            )
            s = lax.dot_general(
                held[0, h * HROWS : (h + 1) * HROWS, :],
                q,
                (((1,), (1,)), ((), ())),
                preferred_element_type=F32,
            )
            top, bottom, cls = s[:128, :128], s[:128, 128:], s[128:129, :128]
            highest = jnp.maximum(jnp.max(jnp.maximum(top, bottom), axis=0, keepdims=True), cls)
            e_top = jnp.exp2((top - highest) * EXP_SCALE)
            e_bottom = jnp.exp2((bottom - highest) * EXP_SCALE)
            e_cls = jnp.exp2((cls - highest) * EXP_SCALE)
            inverse = 1.0 / (jnp.sum(e_top + e_bottom, axis=0, keepdims=True) + e_cls)
            a = jnp.concatenate([e_top * inverse, e_bottom * inverse], axis=1).astype(BF16)
            a_cls = (e_cls * inverse).astype(BF16).astype(F32)
            c = jnp.dot(
                held[1, h * HROWS : h * HROWS + 128, :], a, preferred_element_type=F32
            )
            contexts.append(c[:HD, :128] + c[HD:, 128:] + columns[h] * a_cls)
        pair01 = jnp.concatenate(contexts[0:2], axis=0).T.astype(BF16)
        pair2 = jnp.concatenate([contexts[2], pltpu.roll(contexts[2], 128 - 16, 1)], axis=0).T.astype(BF16)
        for j in range(4):
            result[pairs[j], 0:32, :] = pair01[j * 32 : (j + 1) * 32]
            result[pairs[j], 32:48, :] = pair2[j * 32 : j * 32 + 16]
        return carry

    lax.fori_loop(0, (count + 3) // 4, tile, 0)

    @pl.when(step == 31)
    def _():
        copies = [
            pltpu.make_async_copy(result.at[pl.ds(64 * d, 64)], out_refs[d], sems.at[d])
            for d in range(4)
        ]
        for copy in copies:
            copy.start()
        for copy in copies:
            copy.wait()


def attend(core, image_of, count, table, queries, own, other):
    def at(r):
        return lambda s, *_: (jnp.clip(s - 8 * r, 0, 7), 0, 0)

    whole = pl.BlockSpec((144, 256), lambda s, *_: (0, 0))
    return pl.pallas_call(
        attend_kernel,
        out_shape=[jax.ShapeDtypeStruct((64, 48, 128), BF16)] * 4,
        grid_spec=pltpu.PrefetchScalarGridSpec(
            num_scalar_prefetch=4,
            grid=(32,),
            in_specs=[whole] * 4
            + [pl.BlockSpec((1, BROWS, 128), at(r)) for r in range(4)] * 2,
            out_specs=[pl.BlockSpec(memory_space=pl.ANY)] * 4,
            scratch_shapes=[
                pltpu.VMEM((3, 2, 16, 32, 128), BF16),
                pltpu.VMEM((2, BROWS, 128), BF16),
                pltpu.VMEM((256, 48, 128), BF16),
                pltpu.SemaphoreType.DMA((4,)),
            ],
        ),
        compiler_params=pltpu.CompilerParams(vmem_limit_bytes=40 * 1024 * 1024),
        name="attend",
    )(core, image_of, count, table, *queries, *own, *other)


def finish_kernel(x_ref, c0, c1, c2, c3, weight_ref, states_ref, gain_ref, bias_ref, out_ref, main, low, high):
    @pl.when(pl.program_id(0) == 0)
    def _():
        low[...] = jnp.zeros_like(low)
        high[...] = jnp.zeros_like(high)
        for d in range(4):
            source = lax.rem(x_ref[0] + d, 4)
            main[d * 128 : (d + 1) * 128] = weight_ref[source, 0:128]
            low[d * 128 : d * 128 + 64] = weight_ref[source, 128:192]
            high[d * 128 + 64 : d * 128 + 128] = weight_ref[source, 128:192]

    parts = (c0, c1, c2, c3)
    count = c0.shape[0]
    first = jnp.concatenate([part[:, 0:32, :].reshape(count * 32, 128) for part in parts], axis=1)
    second = jnp.concatenate([part[:, 32:48, :].reshape(count * 16, 128) for part in parts], axis=1)
    mixed = jnp.dot(first, main[...], preferred_element_type=F32).reshape(count, 2, 16, 768)
    early = jnp.dot(second, low[...], preferred_element_type=F32).reshape(count, 16, 768)
    late = jnp.dot(second, high[...], preferred_element_type=F32).reshape(count, 16, 768)
    states = states_ref[0].astype(F32)
    gain = gain_ref[...]
    bias = bias_ref[...]
    for half, extra in ((0, early), (1, late)):
        hidden = mixed[:, half] + extra + states[half * 16 : (half + 1) * 16][None]
        average = jnp.mean(hidden, axis=-1, keepdims=True)
        centered = hidden - average
        variance = jnp.mean(centered * centered, axis=-1, keepdims=True)
        out_ref[0, :, half * 16 : (half + 1) * 16, :] = (
            centered * lax.rsqrt(variance + 1e-06) * gain + bias
        ).astype(BF16)


def finish(x, contexts, output_weight, query_states, gain, bias):
    per_step = 16
    steps = 64 // per_step
    return pl.pallas_call(
        finish_kernel,
        out_shape=jax.ShapeDtypeStruct((4, 16, NQ, 768), BF16),
        grid_spec=pltpu.PrefetchScalarGridSpec(
            num_scalar_prefetch=1,
            grid=(steps,),
            in_specs=[pl.BlockSpec((per_step, 48, 128), lambda s, *_: (s, 0, 0))] * 4
            + [
                pl.BlockSpec((4, 192, 768), lambda s, *_: (0, 0, 0)),
                pl.BlockSpec((1, NQ, 768), lambda s, *_: (s, 0, 0)),
                pl.BlockSpec((1, 768), lambda s, *_: (0, 0)),
                pl.BlockSpec((1, 768), lambda s, *_: (0, 0)),
            ],
            out_specs=pl.BlockSpec((1, 16, NQ, 768), lambda s, *_: (s, 0, 0, 0)),
            scratch_shapes=[pltpu.VMEM((512, 768), BF16)] * 3,
        ),
        compiler_params=pltpu.CompilerParams(vmem_limit_bytes=40 * 1024 * 1024),
        name="finish",
    )(x, *contexts, output_weight.reshape(4, 192, 768), query_states, gain.reshape(1, 768), bias.reshape(1, 768))


def grid_moves(dy, dz):
    return [
        (y * 8 + z, ((y + dy) % 4) * 8 + (z + dz) % 8) for y in range(4) for z in range(8)
    ]


def group_moves(dx, flip=0):
    return [(2 * x + c, 2 * ((x + dx) % 4) + (c ^ flip)) for x in range(4) for c in range(2)]


def on_device(
    caption_embed,
    gallery_embed,
    probe_blocks,
    query_states,
    patches,
    candidates,
    query_weight,
    keyvalue_weight,
    output_weight,
    norm_gain,
    norm_bias,
):
    group_index = lax.axis_index("group")
    shard_index = lax.axis_index("shard")
    x, core = group_index // 2, group_index % 2
    my_y, my_z = shard_index // 8, shard_index % 8
    cap_dev, tokens, model_width = query_states.shape

    def along_shard(value, dy, dz):
        return lax.ppermute(value, "shard", grid_moves(dy, dz))

    def along_group(value, dx, flip=0):
        return lax.ppermute(value, "group", group_moves(dx, flip))

    block = pl.pallas_call(
        project_kernel,
        out_shape=jax.ShapeDtypeStruct((BROWS, 128), BF16),
        in_specs=[
            pl.BlockSpec(memory_space=pltpu.SMEM),
            pl.BlockSpec(memory_space=pltpu.VMEM),
            pl.BlockSpec(memory_space=pltpu.VMEM),
        ],
        out_specs=pl.BlockSpec(memory_space=pltpu.VMEM),
        compiler_params=pltpu.CompilerParams(vmem_limit_bytes=40 * 1024 * 1024),
        name="project",
    )(group_index.reshape(1), patches, keyvalue_weight)
    block = lax.ppermute(
        block, "group", [(k, 2 * k) for k in range(4)] + [(4 + k, 2 * k + 1) for k in range(4)]
    )
    block = lax.dynamic_update_slice(block, caption_embed.reshape(8, 128), (136, 0))

    queries = jnp.dot(
        query_states.reshape(-1, model_width), query_weight, preferred_element_type=F32
    ).astype(BF16)
    ids = candidates.reshape(1, 64).astype(BF16)
    ids = jnp.pad(ids, ((0, 15), (0, 256 - 64)))
    by_chip = jnp.pad(queries.reshape(128, 4, 192), ((0, 0), (0, 0), (0, 64)))

    def message(d):
        rows = lax.dynamic_slice_in_dim(by_chip, (x + d) % 4, 1, axis=1)[:, 0]
        return jnp.concatenate([rows, ids], axis=0)

    received = [message(0)] + [along_group(message(4 - d), 4 - d) for d in (1, 2, 3)]
    pair_images = jnp.concatenate([part[128, :64] for part in received]).astype(jnp.int32)
    numbers = jnp.arange(256, dtype=jnp.int32)
    same = pair_images[:, None] == pair_images[None, :]
    rank = jnp.sum(jnp.logical_and(same, numbers[None, :] < numbers[:, None]), axis=1)
    position = pair_images * SLOTS + rank
    places = jnp.arange(32 * SLOTS, dtype=jnp.int32)
    table = jnp.sum(
        jnp.where(position[None, :] == places[:, None], numbers[None, :], 0), axis=1
    ).astype(jnp.int32)
    count = jnp.sum(
        pair_images[None, :] == jnp.arange(32, dtype=jnp.int32)[:, None], axis=1
    ).astype(jnp.int32)

    half = BROWS // 2
    r1, l1 = along_shard(block, 0, 1), along_shard(block, 0, -1)
    r2, l2 = along_shard(r1, 0, 1), along_shard(l1, 0, -1)
    r3, l3 = along_shard(r2, 0, 1), along_shard(l2, 0, -1)
    r4, l4 = along_shard(r3[:half], 0, 1), along_shard(l3[half:], 0, -1)
    row = jnp.stack([block, r1, l1, r2, l2, r3, l3, jnp.concatenate([r4, l4])])
    rows = [row] + [along_shard(row, d, 0) for d in (1, 2, 3)]
    others = [along_group(part, 0, 1) for part in rows]

    z_shift = jnp.array([0, -1, 1, -2, 2, -3, 3, -4], dtype=jnp.int32)
    y_shift = jnp.array([0, -1, -2, -3], dtype=jnp.int32)
    image_of = (
        ((my_y + y_shift) % 4)[:, None] * 8 + ((my_z + z_shift) % 8)[None, :]
    ).reshape(32)

    sim_scale = 1.0 / (0.07 * math.sqrt(caption_embed.shape[1]))
    group_rows = jnp.concatenate([part[:, 136:144, :] for part in rows]).reshape(128, 256)
    local_blocks = gallery_embed.shape[0] // BLK
    block_ids = shard_index * local_blocks + jnp.arange(local_blocks, dtype=jnp.int32)
    probed = jnp.any(probe_blocks[0][:, None] == block_ids[None, :], axis=0)
    scores = jnp.einsum("ce,re->cr", group_rows, gallery_embed, preferred_element_type=F32) * sim_scale
    scores = scores.reshape(128, local_blocks, BLK)
    is_live = probed[None, :, None]
    masked = jnp.where(is_live, scores, -1e30)
    highest = jnp.max(masked, axis=(1, 2))
    summed = jnp.sum(jnp.where(is_live, jnp.exp(masked - highest[:, None, None]), 0.0), axis=(1, 2))
    partial = jnp.stack([highest.reshape(32, 4), summed.reshape(32, 4)], axis=1)
    order = jnp.arange(32, dtype=jnp.int32)
    pick = image_of[None, :] == order[:, None]
    partial = jnp.sum(jnp.where(pick[:, :, None, None], partial[None], 0.0), axis=1)
    partial = lax.all_to_all(partial, "shard", split_axis=0, concat_axis=0, tiled=True)
    top = jnp.max(partial[:, 0], axis=0)
    normalizer = top + jnp.log(jnp.sum(partial[:, 1] * jnp.exp(partial[:, 0] - top[None]), axis=0))

    contexts = attend(core.reshape(1), image_of, count, table, received, rows, others)
    returned = [contexts[0]] + [along_group(contexts[4 - d], 4 - d) for d in (1, 2, 3)]
    layer_out = finish(x.reshape(1), returned, output_weight, query_states, norm_gain, norm_bias)
    return (layer_out, normalizer)


def solution(mesh):
    placed = (
        P(("group", "shard"), None),
        P("shard", None),
        P("group", None),
        P(("group", "shard"), None, None),
        P("shard", None, None),
        P(("group", "shard"), None, None),
        P(),
        P(None, "group"),
        P(),
        P(),
        P(),
    )
    return jax.shard_map(
        on_device,
        mesh=mesh,
        in_specs=placed,
        out_specs=(P(("group", "shard"), None, None, None), P(("group", "shard"))),
        check_vma=False,
    )
```

```python
import functools
import math

import jax
import jax.numpy as jnp
from jax import lax
from jax.experimental import pallas as pl
from jax.experimental.pallas import tpu as pltpu
from jax.sharding import PartitionSpec as P

HEADS = 12
BLK = 256
HD = 64
NQ = 32
SLOTS = 12
TAIL = 3 * 128
BROWS = TAIL + 16
EXP_SCALE = math.log2(math.e) / math.sqrt(HD)
PARTS = ((0, 64), (64, 64), (128, 64), (192, 64))
F32 = jnp.float32
BF16 = jnp.bfloat16


def in_hbm(value):
    return pltpu.with_memory_space_constraint(value, pltpu.HBM)


def fetched(sources, targets, sems):
    copies = [
        pltpu.make_async_copy(source, target, sems.at[k])
        for k, (source, target) in enumerate(zip(sources, targets))
    ]
    for copy in copies:
        copy.start()
    for copy in copies:
        copy.wait()


def open_kernel(group_ref, *refs):
    candidate_ref, block_ref, messages = refs[6], refs[7], refs[8:12]
    patches_ref, weight_ref, caption_ref, probe_ref, states_ref, ask_ref, sems = refs[12:]
    fetched(refs[:6], refs[12:18], sems)
    across = (((1,), (1,)), ((), ()))
    patches = patches_ref[0]
    weight = weight_ref[...]
    last = lax.dot_general(patches[256:257], weight, across, preferred_element_type=F32)
    pad = jnp.zeros((1, HD), F32)
    captions = caption_ref[...].astype(F32)
    tail = [jnp.concatenate([last[:, h * HD : (h + 1) * HD], pad], axis=1) for h in range(3)]
    tail += [
        lax.shift_right_logical(probe_ref[...], 4).astype(F32),
        (probe_ref[...] & 15).astype(F32),
        jnp.zeros((3, 128), F32),
        captions[:, 0:128],
        captions[:, 128:256],
    ]
    block_ref[TAIL:BROWS, :] = jnp.concatenate(tail).astype(BF16)

    @pl.when(group_ref[0] < 4)
    def _():
        keys = lax.dot_general(patches[:256], weight, across, preferred_element_type=F32)
        for h in range(3):
            block_ref[h * 128 : (h + 1) * 128, 0:HD] = keys[:128, h * HD : (h + 1) * HD].astype(BF16)
            block_ref[h * 128 : (h + 1) * 128, HD:128] = keys[128:, h * HD : (h + 1) * HD].astype(BF16)

    @pl.when(group_ref[0] >= 4)
    def _():
        values = lax.dot_general(weight, patches[:256], across, preferred_element_type=F32)
        for h in range(3):
            rows = values[h * HD : (h + 1) * HD].astype(BF16)
            block_ref[h * 128 : h * 128 + HD] = rows[:, :128]
            block_ref[h * 128 + HD : (h + 1) * 128] = rows[:, 128:]

    queries = jnp.dot(states_ref[...].reshape(128, 768), ask_ref[...], preferred_element_type=F32)
    ids = jnp.concatenate([candidate_ref[c] for c in range(4)], axis=1).astype(F32)
    tail = jnp.concatenate([ids, jnp.zeros((16, 252), F32)], axis=1).astype(BF16)
    pad = jnp.zeros((128, HD), F32)
    x = lax.shift_right_logical(group_ref[0], 1)
    for k in range(4):
        rows = jnp.concatenate([queries[:, k * 192 : (k + 1) * 192], pad], axis=1).astype(BF16)
        for d in range(4):

            @pl.when(((k - x) & 3) == d)
            def _():
                messages[d][0:128, :] = rows

    for d in range(4):
        messages[d][128:144, :] = tail


def opening(group, sources, candidates):
    vmem, hbm = pl.BlockSpec(memory_space=pltpu.VMEM), pl.BlockSpec(memory_space=pltpu.HBM)
    outs = pl.pallas_call(
        open_kernel,
        out_shape=[jax.ShapeDtypeStruct((BROWS, 128), BF16)]
        + [jax.ShapeDtypeStruct((144, 256), BF16)] * 4,
        in_specs=[pl.BlockSpec(memory_space=pltpu.SMEM)] + [hbm] * 6 + [vmem],
        out_specs=[vmem] * 5,
        scratch_shapes=[pltpu.VMEM(source.shape, source.dtype) for source in sources]
        + [pltpu.SemaphoreType.DMA((6,))],
        compiler_params=pltpu.CompilerParams(vmem_limit_bytes=12 * 1024 * 1024),
        name="opening",
    )(group, *[in_hbm(source) for source in sources], candidates)
    return outs[0], outs[1:]


def hold_kernel(*refs):
    pass


def hold(values, after):
    hbm = pl.BlockSpec(memory_space=pltpu.HBM)
    return pl.pallas_call(
        hold_kernel,
        out_shape=[jax.ShapeDtypeStruct(value.shape, value.dtype) for value in values],
        in_specs=[hbm] * (len(values) + len(after)),
        out_specs=[hbm] * len(values),
        input_output_aliases={k: k for k in range(len(values))},
        compiler_params=pltpu.CompilerParams(vmem_limit_bytes=1024 * 1024),
        name="hold",
    )(*[in_hbm(value) for value in values], *after)


def spread_kernel(q0, q1, q2, q3, query):
    left = lax.broadcasted_iota(jnp.int32, (128, 128), 1) < HD
    for d, q_ref in enumerate((q0, q1, q2, q3)):
        rows = q_ref[0:128, :].astype(F32)
        first, second = rows[:, 0:128], rows[:, 128:256]
        turned = pltpu.roll(first, HD, 1)
        parts = (
            (jnp.where(left, first, 0.0), jnp.where(left, 0.0, turned)),
            (jnp.where(left, turned, 0.0), jnp.where(left, 0.0, first)),
            (second, pltpu.roll(second, HD, 1)),
        )
        for h in range(3):
            for side in range(2):
                for c in range(4):
                    query[h, side, d * 4 + c] = parts[h][side][c * 32 : (c + 1) * 32].astype(BF16)


def spread(messages):
    vmem = pl.BlockSpec(memory_space=pltpu.VMEM)
    return pl.pallas_call(
        spread_kernel,
        out_shape=jax.ShapeDtypeStruct((3, 2, 16, NQ, 128), BF16),
        in_specs=[vmem] * 4,
        out_specs=vmem,
        compiler_params=pltpu.CompilerParams(vmem_limit_bytes=8 * 1024 * 1024),
        name="spread",
    )(*messages)


def attend_kernel(sizes, unroll, fresh, final, core_ref, image_ref, count_ref, table_ref, query, *refs):
    parts = len(sizes)
    own_refs, other_refs = refs[:parts], refs[parts : 2 * parts]
    refs = refs[2 * parts + (0 if fresh else 1) :]
    context, token = refs[0:2]
    outs = refs[2:6] if final else ()
    held, column, tiles = refs[2 + len(outs) : 5 + len(outs)]
    images = sum(sizes)
    first_core = core_ref[0] == 0
    total = jnp.int32(0)
    for i in range(images):
        for t in range(3):
            tiles[total + t] = 4 * i + t
        total = total + lax.shift_right_logical(count_ref[image_ref[i]] + 3, 2)
    start = 0
    for part, size in enumerate(sizes):
        for k in range(size):
            mine, theirs = own_refs[part][k], other_refs[part][k]
            held[0, start + k] = jnp.where(first_core, mine, theirs)
            held[1, start + k] = jnp.where(first_core, theirs, mine)
        start += size
    for i in range(images):
        turned = held[1, i, TAIL:BROWS, :].astype(F32).T
        for h in range(3):
            column[i, h] = jnp.broadcast_to(turned[0:HD, h : h + 1], (HD, 128))

    def scores(code):
        i = lax.shift_right_logical(code, 2)
        image = image_ref[i]
        last = count_ref[image] - 1
        first = (code & 3) * 4
        pairs = [table_ref[image * SLOTS + jnp.minimum(first + j, last)] for j in range(4)]
        caps = [lax.shift_right_logical(p, 4) for p in pairs]
        found = []
        for h in range(3):
            q = jnp.concatenate(
                [query[h, 0, c] for c in caps] + [query[h, 1, c] for c in caps], axis=0
            )
            keys = jnp.concatenate([held[0, i, h * 128 : (h + 1) * 128, :], held[0, i, TAIL:BROWS, :]])
            found.append(
                lax.dot_general(
                    keys,
                    q,
                    (((1,), (1,)), ((), ())),
                    preferred_element_type=F32,
                )
            )
        return i, pairs, found

    def mix(i, pairs, found):
        contexts = []
        for h in range(3):
            s = found[h]
            top, bottom, cls = s[:128, :128], s[:128, 128:], s[128 + h : 129 + h, :128]
            highest = jnp.maximum(jnp.max(jnp.maximum(top, bottom), axis=0, keepdims=True), cls)
            e_top = jnp.exp2((top - highest) * EXP_SCALE)
            e_bottom = jnp.exp2((bottom - highest) * EXP_SCALE)
            e_cls = jnp.exp2((cls - highest) * EXP_SCALE)
            inverse = 1.0 / (jnp.sum(e_top + e_bottom, axis=0, keepdims=True) + e_cls)
            a_cls = (e_cls * inverse).astype(BF16).astype(F32)
            a = jnp.concatenate(
                [(e_top * inverse).astype(BF16), (e_bottom * inverse).astype(BF16)], axis=0
            )
            at = h * 128
            v = jnp.concatenate([held[1, i, at : at + HD, :], held[1, i, at + HD : at + 128, :]], axis=1)
            contexts.append(jnp.dot(v, a, preferred_element_type=F32) + column[i, h] * a_cls)
        both = jnp.concatenate(contexts[0:2], axis=0).astype(BF16).T
        third = jnp.concatenate([contexts[2], pltpu.roll(contexts[2], 128 - 16, 1)], axis=0)
        third = third.astype(BF16).T
        for j in range(4):
            context[pairs[j], 0:32, :] = both[j * 32 : (j + 1) * 32]
            context[pairs[j], 32:48, :] = third[j * 32 : j * 32 + 16]

    def group(g, carry):
        codes = [tiles[jnp.minimum(g * unroll + u, total - 1)] for u in range(unroll)]
        for item in [scores(code) for code in codes]:
            mix(*item)
        return carry

    lax.fori_loop(0, lax.div(total + unroll - 1, unroll), group, 0)
    token[...] = jnp.zeros_like(token)
    if final:
        fetched([context.at[pl.ds(at, size)] for at, size in PARTS], outs, refs[-1])


def attend(core, image_of, count, table, query, own, other, context, final):
    sizes = tuple(part.shape[0] for part in own)
    images = sum(sizes)
    fresh = context is None
    smem, vmem = pl.BlockSpec(memory_space=pltpu.SMEM), pl.BlockSpec(memory_space=pltpu.VMEM)
    operands = [core, image_of, count, table, query, *own, *other] + ([] if fresh else [context])
    parts = PARTS if final else ()
    outs = pl.pallas_call(
        functools.partial(attend_kernel, sizes, 5, fresh, final),
        out_shape=[jax.ShapeDtypeStruct((256, 48, 128), BF16), jax.ShapeDtypeStruct((8, 128), F32)]
        + [jax.ShapeDtypeStruct((size, 48, 128), BF16) for _, size in parts],
        in_specs=[smem] * 4 + [vmem] * (len(operands) - 4),
        out_specs=[vmem, vmem] + [pl.BlockSpec(memory_space=pltpu.HBM)] * len(parts),
        input_output_aliases={} if fresh else {len(operands) - 1: 0},
        scratch_shapes=[
            pltpu.VMEM((2, images, BROWS, 128), BF16),
            pltpu.VMEM((images, 3, HD, 128), F32),
            pltpu.SMEM((images * 3 + 4,), jnp.int32),
        ]
        + ([pltpu.SemaphoreType.DMA((4,))] if final else []),
        cost_estimate=pl.CostEstimate(
            flops=images * 600_000_000, bytes_accessed=images * 800_000, transcendentals=images * 800_000
        ),
        compiler_params=pltpu.CompilerParams(vmem_limit_bytes=14 * 1024 * 1024),
        name="attend",
    )(*operands)
    return outs[0], outs[1], outs[2:]


def score_kernel(shard_ref, *refs):
    count = len(refs) - 6
    pieces, gallery, out_ref = refs[:count], refs[count], refs[count + 1]
    tails, rows, scores, sems = refs[count + 2 :]
    copies = [pltpu.make_async_copy(gallery, rows, sems.at[count])]
    start = 0
    for k, piece in enumerate(pieces):
        images = piece.shape[0]
        copies.append(
            pltpu.make_async_copy(
                piece.at[:, pl.ds(TAIL, 16), :], tails.at[pl.ds(start, images)], sems.at[k]
            )
        )
        start += images
    for copy in copies:
        copy.start()
    for copy in copies:
        copy.wait()
    scale = 1.0 / (0.07 * math.sqrt(256))
    first, second = [], []
    for i in range(32):
        tail = tails[i].astype(F32)
        first.append(tail[8:12])
        second.append(tail[12:16])
    captions = jnp.concatenate([jnp.concatenate(first), jnp.concatenate(second)], axis=1).astype(BF16)
    tail = tails[0].astype(F32)
    near = tail[3:4] == shard_ref[0].astype(F32)
    highest = jnp.full((8, 128), -1e30, F32)
    alive = []
    for b in range(16):
        hit = jnp.where(jnp.logical_and(near, tail[4:5] == float(b)), 1.0, 0.0)
        alive.append(jnp.broadcast_to(jnp.max(hit, axis=1, keepdims=True), (8, 128)) > 0.5)
        s = lax.dot_general(
            rows[b * BLK : (b + 1) * BLK], captions, (((1,), (1,)), ((), ())), preferred_element_type=F32
        )
        s = s * scale
        scores[b] = s
        most = jnp.max(s.reshape(BLK // 8, 8, 128), axis=0)
        highest = jnp.maximum(highest, jnp.where(alive[b], most, -1e30))
    top = jnp.max(highest, axis=0, keepdims=True)
    total = jnp.zeros((8, 128), F32)
    for b in range(16):
        e = jnp.sum(jnp.exp(scores[b] - top).reshape(BLK // 8, 8, 128), axis=0)
        total = total + jnp.where(alive[b], e, 0.0)
    out_ref[0:1, :] = top
    out_ref[1:2, :] = jnp.sum(total, axis=0, keepdims=True)


def score(shard, pieces, gallery):
    hbm = pl.BlockSpec(memory_space=pltpu.HBM)
    return pl.pallas_call(
        score_kernel,
        out_shape=jax.ShapeDtypeStruct((2, 128), F32),
        in_specs=[pl.BlockSpec(memory_space=pltpu.SMEM)] + [hbm] * (len(pieces) + 1),
        out_specs=pl.BlockSpec(memory_space=pltpu.VMEM),
        scratch_shapes=[
            pltpu.VMEM((32, 16, 128), BF16),
            pltpu.VMEM(gallery.shape, BF16),
            pltpu.VMEM((16, BLK, 128), F32),
            pltpu.SemaphoreType.DMA((len(pieces) + 1,)),
        ],
        cost_estimate=pl.CostEstimate(flops=1000, bytes_accessed=1000, transcendentals=0),
        compiler_params=pltpu.CompilerParams(vmem_limit_bytes=12 * 1024 * 1024),
        name="score",
    )(shard, *pieces, gallery)


def finish_kernel(x_ref, c0, c1, c2, c3, weight_ref, states_ref, gain_ref, bias_ref, out_ref, main, low, high):
    @pl.when(pl.program_id(0) == 0)
    def _():
        low[...] = jnp.zeros_like(low)
        high[...] = jnp.zeros_like(high)
        for d in range(4):
            source = lax.rem(x_ref[0] + d, 4)
            main[d * 128 : (d + 1) * 128] = weight_ref[source, 0:128]
            low[d * 128 : d * 128 + 64] = weight_ref[source, 128:192]
            high[d * 128 + 64 : d * 128 + 128] = weight_ref[source, 128:192]

    parts = (c0, c1, c2, c3)
    count = c0.shape[0]
    first = jnp.concatenate([part[:, 0:32, :].reshape(count * 32, 128) for part in parts], axis=1)
    second = jnp.concatenate([part[:, 32:48, :].reshape(count * 16, 128) for part in parts], axis=1)
    mixed = jnp.dot(first, main[...], preferred_element_type=F32).reshape(count, 2, 16, 768)
    early = jnp.dot(second, low[...], preferred_element_type=F32).reshape(count, 16, 768)
    late = jnp.dot(second, high[...], preferred_element_type=F32).reshape(count, 16, 768)
    states = states_ref[0].astype(F32)
    gain = gain_ref[...]
    bias = bias_ref[...]
    for half, extra in ((0, early), (1, late)):
        hidden = mixed[:, half] + extra + states[half * 16 : (half + 1) * 16][None]
        average = jnp.mean(hidden, axis=-1, keepdims=True)
        centered = hidden - average
        variance = jnp.mean(centered * centered, axis=-1, keepdims=True)
        out_ref[0, :, half * 16 : (half + 1) * 16, :] = (
            centered * lax.rsqrt(variance + 1e-06) * gain + bias
        ).astype(BF16)


def finish(x, contexts, output_weight, query_states, gain, bias):
    per_step = 16
    each = pl.BlockSpec((per_step, 48, 128), lambda s, *_: (s, 0, 0))
    return pl.pallas_call(
        finish_kernel,
        out_shape=jax.ShapeDtypeStruct((4, 16, NQ, 768), BF16),
        grid_spec=pltpu.PrefetchScalarGridSpec(
            num_scalar_prefetch=1,
            grid=(64 // per_step,),
            in_specs=[each] * 4
            + [
                pl.BlockSpec((4, 192, 768), lambda s, *_: (0, 0, 0)),
                pl.BlockSpec((1, NQ, 768), lambda s, *_: (s, 0, 0)),
                pl.BlockSpec((1, 768), lambda s, *_: (0, 0)),
                pl.BlockSpec((1, 768), lambda s, *_: (0, 0)),
            ],
            out_specs=pl.BlockSpec((1, 16, NQ, 768), lambda s, *_: (s, 0, 0, 0)),
            scratch_shapes=[pltpu.VMEM((512, 768), BF16)] * 3,
        ),
        compiler_params=pltpu.CompilerParams(vmem_limit_bytes=32 * 1024 * 1024),
        name="finish",
    )(x, *contexts, output_weight.reshape(4, 192, 768), query_states, gain.reshape(1, 768), bias.reshape(1, 768))


def grid_moves(dy, dz):
    return [
        (y * 8 + z, ((y + dy) % 4) * 8 + (z + dz) % 8) for y in range(4) for z in range(8)
    ]


def group_moves(dx, flip=0):
    return [(2 * x + c, 2 * ((x + dx) % 4) + (c ^ flip)) for x in range(4) for c in range(2)]


def on_device(
    caption_embed,
    gallery_embed,
    probe_blocks,
    query_states,
    patches,
    candidates,
    query_weight,
    keyvalue_weight,
    output_weight,
    norm_gain,
    norm_bias,
):
    group_index = lax.axis_index("group")
    shard_index = lax.axis_index("shard")
    x, core = group_index // 2, group_index % 2
    my_y, my_z = shard_index // 8, shard_index % 8
    cap_dev, tokens, model_width = query_states.shape

    def along_shard(value, dy, dz):
        return lax.ppermute(value, "shard", grid_moves(dy, dz))

    def along_group(value, dx, flip=0):
        return lax.ppermute(value, "group", group_moves(dx, flip))

    sources = [patches, keyvalue_weight.T, caption_embed, probe_blocks, query_states, query_weight]
    block, messages = opening(group_index.reshape(1), sources, candidates)
    homes = [(k, 2 * k) for k in range(4)] + [(4 + k, 2 * k + 1) for k in range(4)]

    def homeward(dy):
        moves = [(g * 32 + a, h * 32 + b) for g, h in homes for a, b in grid_moves(dy, 0)]
        return lax.ppermute(block, ("group", "shard"), moves)

    arrived = [homeward(dy) for dy in range(4)]
    received = [messages[0]] + [along_group(messages[4 - d], 4 - d) for d in (1, 2, 3)]
    stack = jnp.stack(arrived)
    pair_images = jnp.stack([part[128:144, :4].T for part in received]).reshape(256).astype(jnp.int32)
    numbers = jnp.arange(256, dtype=jnp.int32)
    same = pair_images[:, None] == pair_images[None, :]
    rank = jnp.sum(jnp.logical_and(same, numbers[None, :] < numbers[:, None]), axis=1)
    position = pair_images * SLOTS + rank
    places = jnp.arange(32 * SLOTS, dtype=jnp.int32)
    table = jnp.sum(
        jnp.where(position[None, :] == places[:, None], numbers[None, :], 0), axis=1
    ).astype(jnp.int32)
    count = jnp.sum(
        pair_images[None, :] == jnp.arange(32, dtype=jnp.int32)[:, None], axis=1
    ).astype(jnp.int32)

    query = spread(received)
    def images(y_shifts, z_shift):
        return [((my_y - dy) % 4) * 8 + (my_z - z_shift) % 8 for dy in y_shifts]

    whole = (0, 1, 2, 3)
    piece_images = [images(whole, 0)]
    piece_images += [images(whole, k) + images(whole, -k) for k in (1, 2, 3)]
    piece_images += [images((0, 1), 4) + images((2, 3), -4)]
    piece_images = [jnp.stack(part).astype(jnp.int32) for part in piece_images]
    image_of = jnp.concatenate(piece_images)

    pieces = [[stack]]
    context = None
    right = left = stack
    for step in range(5):
        if step < 3:
            coming = [along_shard(right, 0, 1), along_shard(left, 0, -1)]
        elif step == 3:
            coming = [along_shard(right[:2], 0, 1), along_shard(left[2:], 0, -1)]
        own = pieces[-1]
        other = [along_group(part, 0, 1) for part in own]
        context, token, outs = attend(
            core.reshape(1), piece_images[step], count, table, query, own, other, context, step == 4
        )
        if step < 4:
            right, left = coming
            pieces.append([right, left])

    sent = [outs[0]] + [along_group(outs[4 - d], 4 - d) for d in (1, 2, 3)]

    partial = score(shard_index.reshape(1), [part for own in pieces for part in own], gallery_embed)
    order = jnp.arange(32, dtype=jnp.int32)
    pick = image_of[None, :] == order[:, None]
    partial = partial.reshape(2, 32, 4)
    partial = jnp.sum(jnp.where(pick[:, None, :, None], partial[None], 0.0), axis=2)
    partial = lax.all_to_all(partial, "shard", split_axis=0, concat_axis=0, tiled=True)
    top = jnp.max(partial[:, 0], axis=0)
    normalizer = top + jnp.log(jnp.sum(partial[:, 1] * jnp.exp(partial[:, 0] - top[None]), axis=0))
    normalizer = hold([jnp.pad(normalizer.reshape(1, 4), ((0, 7), (0, 124)))], sent[1:])[0]
    normalizer = lax.ppermute(normalizer, "group", [(h, g) for g, h in homes])[0, :4]

    layer_out = finish(x.reshape(1), sent, output_weight, query_states, norm_gain, norm_bias)
    return (layer_out, normalizer)


def solution(mesh):
    placed = (
        P(("group", "shard"), None),
        P("shard", None),
        P("group", None),
        P(("group", "shard"), None, None),
        P("shard", None, None),
        P(("group", "shard"), None, None),
        P(),
        P(None, "group"),
        P(),
        P(),
        P(),
    )
    return jax.shard_map(
        on_device,
        mesh=mesh,
        in_specs=placed,
        out_specs=(P(("group", "shard"), None, None, None), P(("group", "shard"))),
        check_vma=False,
    )
```

```python
import functools
import math

import jax
import jax.numpy as jnp
from jax import lax
from jax.experimental import pallas as pl
from jax.experimental.pallas import tpu as pltpu
from jax.sharding import PartitionSpec as P

HEADS = 12
BLK = 256
HD = 64
NQ = 32
SLOTS = 12
TAIL = 3 * 128
BROWS = TAIL + 16
EXP_SCALE = math.log2(math.e) / math.sqrt(HD)
PARTS = ((64, 64), (128, 64), (192, 64))
IMAGE_AT, COUNT_AT, TABLE_AT = 1, 33, 65
F32 = jnp.float32
BF16 = jnp.bfloat16


def in_hbm(value):
    return pltpu.with_memory_space_constraint(value, pltpu.HBM)


def fetched(sources, targets, sems):
    copies = [
        pltpu.make_async_copy(source, target, sems.at[k])
        for k, (source, target) in enumerate(zip(sources, targets))
    ]
    for copy in copies:
        copy.start()
    for copy in copies:
        copy.wait()


def open_kernel(group_ref, *refs):
    candidate_ref, block_ref, messages = refs[6], refs[7], refs[8:12]
    patches_ref, weight_ref, caption_ref, probe_ref, states_ref, ask_ref, sems = refs[12:]
    fetched(refs[:6], refs[12:18], sems)
    across = (((1,), (1,)), ((), ()))
    patches = patches_ref[0]
    weight = weight_ref[...]
    last = lax.dot_general(patches[256:257], weight, across, preferred_element_type=F32)
    pad = jnp.zeros((1, HD), F32)
    captions = caption_ref[...].astype(F32)
    tail = [jnp.concatenate([last[:, h * HD : (h + 1) * HD], pad], axis=1) for h in range(3)]
    tail += [
        lax.shift_right_logical(probe_ref[...], 4).astype(F32),
        (probe_ref[...] & 15).astype(F32),
        jnp.zeros((3, 128), F32),
        captions[:, 0:128],
        captions[:, 128:256],
    ]
    block_ref[TAIL:BROWS, :] = jnp.concatenate(tail).astype(BF16)

    @pl.when(group_ref[0] < 4)
    def _():
        keys = lax.dot_general(patches[:256], weight, across, preferred_element_type=F32)
        for h in range(3):
            block_ref[h * 128 : (h + 1) * 128, 0:HD] = keys[:128, h * HD : (h + 1) * HD].astype(BF16)
            block_ref[h * 128 : (h + 1) * 128, HD:128] = keys[128:, h * HD : (h + 1) * HD].astype(BF16)

    @pl.when(group_ref[0] >= 4)
    def _():
        values = lax.dot_general(weight, patches[:256], across, preferred_element_type=F32)
        for h in range(3):
            rows = values[h * HD : (h + 1) * HD].astype(BF16)
            block_ref[h * 128 : h * 128 + HD] = rows[:, :128]
            block_ref[h * 128 + HD : (h + 1) * 128] = rows[:, 128:]

    queries = jnp.dot(states_ref[...].reshape(128, 768), ask_ref[...], preferred_element_type=F32)
    ids = jnp.concatenate([candidate_ref[c] for c in range(4)], axis=1).astype(F32)
    tail = jnp.concatenate([ids, jnp.zeros((16, 252), F32)], axis=1).astype(BF16)
    pad = jnp.zeros((128, HD), F32)
    x = lax.shift_right_logical(group_ref[0], 1)
    for k in range(4):
        rows = jnp.concatenate([queries[:, k * 192 : (k + 1) * 192], pad], axis=1).astype(BF16)
        for d in range(4):

            @pl.when(((k - x) & 3) == d)
            def _():
                messages[d][0:128, :] = rows

    for d in range(4):
        messages[d][128:144, :] = tail


def opening(group, sources, candidates):
    vmem, hbm = pl.BlockSpec(memory_space=pltpu.VMEM), pl.BlockSpec(memory_space=pltpu.HBM)
    outs = pl.pallas_call(
        open_kernel,
        out_shape=[jax.ShapeDtypeStruct((BROWS, 128), BF16)]
        + [jax.ShapeDtypeStruct((144, 256), BF16)] * 4,
        in_specs=[pl.BlockSpec(memory_space=pltpu.SMEM)] + [hbm] * 6 + [vmem],
        out_specs=[vmem] * 5,
        scratch_shapes=[pltpu.VMEM(source.shape, source.dtype) for source in sources]
        + [pltpu.SemaphoreType.DMA((7,))],
        compiler_params=pltpu.CompilerParams(vmem_limit_bytes=12 * 1024 * 1024),
        name="opening",
    )(group, *[in_hbm(source) for source in sources], candidates)
    return outs[0], outs[1:]


def hold_kernel(*refs):
    pass


def hold(values, after, near=0):
    anywhere, vmem = pl.BlockSpec(memory_space=pl.ANY), pl.BlockSpec(memory_space=pltpu.VMEM)
    specs = [anywhere] * (len(values) - near) + [vmem] * near
    return pl.pallas_call(
        hold_kernel,
        out_shape=[jax.ShapeDtypeStruct(value.shape, value.dtype) for value in values],
        in_specs=specs + [anywhere] * len(after),
        out_specs=specs,
        input_output_aliases={k: k for k in range(len(values))},
        compiler_params=pltpu.CompilerParams(vmem_limit_bytes=1024 * 1024),
        name="hold",
    )(*values, *after)


def spread_kernel(q0, q1, q2, q3, query):
    left = lax.broadcasted_iota(jnp.int32, (128, 128), 1) < HD
    for d, q_ref in enumerate((q0, q1, q2, q3)):
        rows = q_ref[0:128, :].astype(F32)
        first, second = rows[:, 0:128], rows[:, 128:256]
        turned = pltpu.roll(first, HD, 1)
        parts = (
            (jnp.where(left, first, 0.0), jnp.where(left, 0.0, turned)),
            (jnp.where(left, turned, 0.0), jnp.where(left, 0.0, first)),
            (second, pltpu.roll(second, HD, 1)),
        )
        for h in range(3):
            for side in range(2):
                for c in range(4):
                    query[h, side, d * 4 + c] = parts[h][side][c * 32 : (c + 1) * 32].astype(BF16)


def spread(messages):
    vmem = pl.BlockSpec(memory_space=pltpu.VMEM)
    return pl.pallas_call(
        spread_kernel,
        out_shape=jax.ShapeDtypeStruct((3, 2, 16, NQ, 128), BF16),
        in_specs=[vmem] * 4,
        out_specs=vmem,
        compiler_params=pltpu.CompilerParams(vmem_limit_bytes=8 * 1024 * 1024),
        name="spread",
    )(*messages)


def attend_kernel(sizes, first_image, unroll, fresh, final, plan_ref, query_ref, *refs):
    parts = len(sizes)
    own_refs, other_refs = refs[:parts], refs[parts : 2 * parts]
    refs = refs[2 * parts + (0 if fresh else 1) :]
    context = refs[0]
    outs = refs[1:4] if final else ()
    query, held, column, tiles, sems = refs[1 + len(outs) :]
    images = sum(sizes)
    core = plan_ref[0]
    copies = [pltpu.make_async_copy(query_ref, query, sems.at[2 * parts])]
    start = 0
    for part, size in enumerate(sizes):
        for k, (source, kind) in enumerate(((own_refs[part], core), (other_refs[part], 1 - core))):
            target = held.at[kind, pl.ds(start, size)]
            copies.append(pltpu.make_async_copy(source, target, sems.at[2 * part + k]))
        start += size
    for copy in copies:
        copy.start()
    total = jnp.int32(0)
    for i in range(images):
        for t in range(3):
            tiles[total + t] = 4 * i + t
        amount = plan_ref[COUNT_AT + plan_ref[IMAGE_AT + first_image + i]]
        total = total + lax.shift_right_logical(amount + 3, 2)
    for copy in copies:
        copy.wait()
    for i in range(images):
        turned = held[1, i, TAIL:BROWS, :].astype(F32).T
        for h in range(3):
            column[i, h] = jnp.broadcast_to(turned[0:HD, h : h + 1], (HD, 128))

    def scores(code):
        i = lax.shift_right_logical(code, 2)
        image = plan_ref[IMAGE_AT + first_image + i]
        last = plan_ref[COUNT_AT + image] - 1
        first = (code & 3) * 4
        pairs = [plan_ref[TABLE_AT + image * SLOTS + jnp.minimum(first + j, last)] for j in range(4)]
        caps = [lax.shift_right_logical(p, 4) for p in pairs]
        found = []
        for h in range(3):
            q = jnp.concatenate(
                [query[h, 0, c] for c in caps] + [query[h, 1, c] for c in caps], axis=0
            )
            keys = jnp.concatenate([held[0, i, h * 128 : (h + 1) * 128, :], held[0, i, TAIL:BROWS, :]])
            found.append(
                lax.dot_general(
                    keys,
                    q,
                    (((1,), (1,)), ((), ())),
                    preferred_element_type=F32,
                )
            )
        return i, pairs, found

    def mix(i, pairs, found):
        contexts = []
        for h in range(3):
            s = found[h]
            top, bottom, cls = s[:128, :128], s[:128, 128:], s[128 + h : 129 + h, :128]
            highest = jnp.maximum(jnp.max(jnp.maximum(top, bottom), axis=0, keepdims=True), cls)
            e_top = jnp.exp2((top - highest) * EXP_SCALE)
            e_bottom = jnp.exp2((bottom - highest) * EXP_SCALE)
            e_cls = jnp.exp2((cls - highest) * EXP_SCALE)
            inverse = 1.0 / (jnp.sum(e_top + e_bottom, axis=0, keepdims=True) + e_cls)
            a_cls = (e_cls * inverse).astype(BF16).astype(F32)
            a = jnp.concatenate(
                [(e_top * inverse).astype(BF16), (e_bottom * inverse).astype(BF16)], axis=0
            )
            at = h * 128
            v = jnp.concatenate([held[1, i, at : at + HD, :], held[1, i, at + HD : at + 128, :]], axis=1)
            contexts.append(jnp.dot(v, a, preferred_element_type=F32) + column[i, h] * a_cls)
        both = jnp.concatenate(contexts[0:2], axis=0).astype(BF16).T
        third = jnp.concatenate([contexts[2], pltpu.roll(contexts[2], 128 - 16, 1)], axis=0)
        third = third.astype(BF16).T
        for j in range(4):
            context[pairs[j], 0:32, :] = both[j * 32 : (j + 1) * 32]
            context[pairs[j], 32:48, :] = third[j * 32 : j * 32 + 16]

    def group(g, carry):
        codes = [tiles[jnp.minimum(g * unroll + u, total - 1)] for u in range(unroll)]
        for item in [scores(code) for code in codes]:
            mix(*item)
        return carry

    lax.fori_loop(0, lax.div(total + unroll - 1, unroll), group, 0)
    if final:
        fetched([context.at[pl.ds(at, size)] for at, size in PARTS], outs, sems)


def attend(plan, first_image, query, own, other, context, final):
    sizes = tuple(part.shape[0] for part in own)
    images = sum(sizes)
    fresh = context is None
    vmem, anywhere = pl.BlockSpec(memory_space=pltpu.VMEM), pl.BlockSpec(memory_space=pl.ANY)
    pieces = [*own, *[in_hbm(part) for part in other]]
    operands = [in_hbm(plan), in_hbm(query), *pieces] + ([] if fresh else [context])
    parts = PARTS if final else ()
    outs = pl.pallas_call(
        functools.partial(attend_kernel, sizes, first_image, 5, fresh, final),
        out_shape=[jax.ShapeDtypeStruct((256, 48, 128), BF16)]
        + [jax.ShapeDtypeStruct((size, 48, 128), BF16) for _, size in parts],
        in_specs=[pl.BlockSpec(memory_space=pltpu.SMEM)]
        + [anywhere] * (1 + len(pieces))
        + ([] if fresh else [vmem]),
        out_specs=[vmem] + [pl.BlockSpec(memory_space=pltpu.HBM)] * len(parts),
        input_output_aliases={} if fresh else {len(operands) - 1: 0},
        scratch_shapes=[
            pltpu.VMEM(query.shape, BF16),
            pltpu.VMEM((2, images, BROWS, 128), BF16),
            pltpu.VMEM((images, 3, HD, 128), F32),
            pltpu.SMEM((images * 3 + 4,), jnp.int32),
            pltpu.SemaphoreType.DMA((7,)),
        ],
        cost_estimate=pl.CostEstimate(
            flops=images * 600_000_000, bytes_accessed=images * 800_000, transcendentals=images * 800_000
        ),
        compiler_params=pltpu.CompilerParams(vmem_limit_bytes=14 * 1024 * 1024),
        name="attend",
    )(*operands)
    return outs[0], outs[1:]


def score_kernel(shard_ref, *refs):
    count = len(refs) - 10
    pieces, gallery, context = refs[:count], refs[count], refs[count + 1]
    out_ref, kept, tails, rows, scores, sems = refs[count + 4 :]
    copies = [
        pltpu.make_async_copy(gallery, rows, sems.at[count]),
        pltpu.make_async_copy(context.at[pl.ds(0, 64)], kept, sems.at[count + 1]),
    ]
    start = 0
    for k, piece in enumerate(pieces):
        images = piece.shape[0]
        copies.append(
            pltpu.make_async_copy(
                piece.at[:, pl.ds(TAIL, 16), :], tails.at[pl.ds(start, images)], sems.at[k]
            )
        )
        start += images
    for copy in copies:
        copy.start()
    for copy in copies:
        copy.wait()
    scale = 1.0 / (0.07 * math.sqrt(256))
    first, second = [], []
    for i in range(32):
        tail = tails[i].astype(F32)
        first.append(tail[8:12])
        second.append(tail[12:16])
    captions = jnp.concatenate([jnp.concatenate(first), jnp.concatenate(second)], axis=1).astype(BF16)
    tail = tails[0].astype(F32)
    near = tail[3:4] == shard_ref[0].astype(F32)
    highest = jnp.full((8, 128), -1e30, F32)
    alive = []
    for b in range(16):
        hit = jnp.where(jnp.logical_and(near, tail[4:5] == float(b)), 1.0, 0.0)
        alive.append(jnp.broadcast_to(jnp.max(hit, axis=1, keepdims=True), (8, 128)) > 0.5)
        s = lax.dot_general(
            rows[b * BLK : (b + 1) * BLK], captions, (((1,), (1,)), ((), ())), preferred_element_type=F32
        )
        s = s * scale
        scores[b] = s
        most = jnp.max(s.reshape(BLK // 8, 8, 128), axis=0)
        highest = jnp.maximum(highest, jnp.where(alive[b], most, -1e30))
    top = jnp.max(highest, axis=0, keepdims=True)
    total = jnp.zeros((8, 128), F32)
    for b in range(16):
        e = jnp.sum(jnp.exp(scores[b] - top).reshape(BLK // 8, 8, 128), axis=0)
        total = total + jnp.where(alive[b], e, 0.0)
    out_ref[0:1, :] = top
    out_ref[1:2, :] = jnp.sum(total, axis=0, keepdims=True)


def score(shard, pieces, gallery, context, ready):
    hbm, vmem, anywhere = (pl.BlockSpec(memory_space=space) for space in (pltpu.HBM, pltpu.VMEM, pl.ANY))
    return pl.pallas_call(
        score_kernel,
        out_shape=[jax.ShapeDtypeStruct((2, 128), F32), jax.ShapeDtypeStruct((64, 48, 128), BF16)],
        in_specs=[pl.BlockSpec(memory_space=pltpu.SMEM)] + [anywhere] * (len(pieces) + 1) + [vmem] + [anywhere] * len(ready),
        out_specs=[vmem, hbm],
        scratch_shapes=[
            pltpu.VMEM((32, 16, 128), BF16),
            pltpu.VMEM(gallery.shape, BF16),
            pltpu.VMEM((16, BLK, 128), F32),
            pltpu.SemaphoreType.DMA((len(pieces) + 2,)),
        ],
        cost_estimate=pl.CostEstimate(flops=1000, bytes_accessed=1000, transcendentals=0),
        compiler_params=pltpu.CompilerParams(vmem_limit_bytes=12 * 1024 * 1024),
        name="score",
    )(shard, *pieces, gallery, context, *ready)


def finish_kernel(x_ref, c0, c1, c2, c3, weight_ref, states_ref, gain_ref, bias_ref, out_ref, main, third):
    @pl.when(pl.program_id(0) == 0)
    def _():
        for d in range(4):
            source = lax.rem(x_ref[0] + d, 4)
            main[d * 128 : (d + 1) * 128] = weight_ref[source, 0:128]
            third[d * 64 : (d + 1) * 64] = weight_ref[source, 128:192]

    parts = (c0, c1, c2, c3)
    count = c0.shape[0]
    first = jnp.concatenate([part[:, 0:32, :].reshape(count * 32, 128) for part in parts], axis=1)
    second = [part[:, 32:48, :].reshape(count * 16, 128) for part in parts]
    left = lax.broadcasted_iota(jnp.int32, second[0].shape, 1) < HD
    pairs = ((second[0], second[1]), (second[2], second[3]))
    lows = [jnp.where(left, one, jnp.concatenate([two[:, HD:], two[:, :HD]], axis=1)) for one, two in pairs]
    highs = [jnp.where(left, jnp.concatenate([one[:, HD:], one[:, :HD]], axis=1), two) for one, two in pairs]
    mixed = jnp.dot(first, main[...], preferred_element_type=F32).reshape(count, 2, 16, 768)
    early = jnp.dot(jnp.concatenate(lows, axis=1), third[...], preferred_element_type=F32).reshape(count, 16, 768)
    late = jnp.dot(jnp.concatenate(highs, axis=1), third[...], preferred_element_type=F32).reshape(count, 16, 768)
    states = states_ref[0].astype(F32)
    gain = gain_ref[...]
    bias = bias_ref[...]
    for half, extra in ((0, early), (1, late)):
        hidden = mixed[:, half] + extra + states[half * 16 : (half + 1) * 16][None]
        average = jnp.mean(hidden, axis=-1, keepdims=True)
        centered = hidden - average
        variance = jnp.mean(centered * centered, axis=-1, keepdims=True)
        out_ref[0, :, half * 16 : (half + 1) * 16, :] = (
            centered * lax.rsqrt(variance + 1e-06) * gain + bias
        ).astype(BF16)


def finish(x, contexts, output_weight, query_states, gain, bias):
    per_step = 16
    each = pl.BlockSpec((per_step, 48, 128), lambda s, *_: (s, 0, 0))
    return pl.pallas_call(
        finish_kernel,
        out_shape=jax.ShapeDtypeStruct((4, 16, NQ, 768), BF16),
        grid_spec=pltpu.PrefetchScalarGridSpec(
            num_scalar_prefetch=1,
            grid=(64 // per_step,),
            in_specs=[each] * 4
            + [
                pl.BlockSpec((4, 192, 768), lambda s, *_: (0, 0, 0)),
                pl.BlockSpec((1, NQ, 768), lambda s, *_: (s, 0, 0)),
                pl.BlockSpec((1, 768), lambda s, *_: (0, 0)),
                pl.BlockSpec((1, 768), lambda s, *_: (0, 0)),
            ],
            out_specs=pl.BlockSpec((1, 16, NQ, 768), lambda s, *_: (s, 0, 0, 0)),
            scratch_shapes=[pltpu.VMEM((512, 768), BF16), pltpu.VMEM((256, 768), BF16)],
        ),
        compiler_params=pltpu.CompilerParams(vmem_limit_bytes=32 * 1024 * 1024),
        name="finish",
    )(x, *[in_hbm(part) for part in (*contexts, output_weight.reshape(4, 192, 768), query_states, gain, bias)])


def grid_moves(dy, dz):
    return [
        (y * 8 + z, ((y + dy) % 4) * 8 + (z + dz) % 8) for y in range(4) for z in range(8)
    ]


def group_moves(dx, flip=0):
    return [(2 * x + c, 2 * ((x + dx) % 4) + (c ^ flip)) for x in range(4) for c in range(2)]


def on_device(
    caption_embed,
    gallery_embed,
    probe_blocks,
    query_states,
    patches,
    candidates,
    query_weight,
    keyvalue_weight,
    output_weight,
    norm_gain,
    norm_bias,
):
    group_index = lax.axis_index("group")
    shard_index = lax.axis_index("shard")
    x, core = group_index // 2, group_index % 2
    my_y, my_z = shard_index // 8, shard_index % 8
    cap_dev, tokens, model_width = query_states.shape

    def along_shard(value, dy, dz):
        return lax.ppermute(value, "shard", grid_moves(dy, dz))

    def along_group(value, dx, flip=0):
        return lax.ppermute(value, "group", group_moves(dx, flip))

    sources = [patches, keyvalue_weight.T, caption_embed, probe_blocks, query_states, query_weight]
    block, messages = opening(group_index.reshape(1), sources, candidates)
    homes = [(k, 2 * k) for k in range(4)] + [(4 + k, 2 * k + 1) for k in range(4)]

    def homeward(dy):
        moves = [(g * 32 + a, h * 32 + b) for g, h in homes for a, b in grid_moves(dy, 0)]
        return lax.ppermute(block, ("group", "shard"), moves)

    arrived = [homeward(dy) for dy in range(4)]
    messages = hold(messages, arrived[:2])
    received = [messages[0]] + [along_group(messages[4 - d], 4 - d) for d in (1, 2, 3)]
    stack = jnp.stack(arrived)
    pair_images = jnp.stack([part[128:144, :4].T for part in received]).reshape(256).astype(jnp.int32)
    numbers = jnp.arange(256, dtype=jnp.int32)
    same = pair_images[:, None] == pair_images[None, :]
    rank = jnp.sum(jnp.logical_and(same, numbers[None, :] < numbers[:, None]), axis=1)
    position = pair_images * SLOTS + rank
    places = jnp.arange(32 * SLOTS, dtype=jnp.int32)
    table = jnp.sum(
        jnp.where(position[None, :] == places[:, None], numbers[None, :], 0), axis=1
    ).astype(jnp.int32)
    count = jnp.sum(
        pair_images[None, :] == jnp.arange(32, dtype=jnp.int32)[:, None], axis=1
    ).astype(jnp.int32)

    query = spread(received)
    def images(y_shifts, z_shift):
        return [((my_y - dy) % 4) * 8 + (my_z - z_shift) % 8 for dy in y_shifts]

    whole = (0, 1, 2, 3)
    arrivals = images(whole, 0)
    for k in (1, 2, 3):
        arrivals += images(whole, k) + images(whole, -k)
    arrivals += images((0, 1), 4) + images((2, 3), -4)
    image_of = jnp.stack(arrivals).astype(jnp.int32)
    plan = jnp.concatenate([core.reshape(1).astype(jnp.int32), image_of, count, table, jnp.zeros((63,), jnp.int32)])

    pieces = [[stack]]
    waiting = []
    context, first_image = None, 0
    right = left = stack
    for step in range(5):
        if step < 3:
            coming = [along_shard(right, 0, 1), along_shard(left, 0, -1)]
        elif step == 3:
            coming = [along_shard(right[:2], 0, 1), along_shard(left[2:], 0, -1)]
        waiting += pieces[-1]
        if step > 0:
            other = [along_group(part, 0, 1) for part in waiting]
            context, outs = attend(plan, first_image, query, waiting, other, context, step == 4)
            first_image += sum(part.shape[0] for part in waiting)
            waiting = []
        if step < 4:
            right, left = coming
            if step > 0:
                right, left, context = hold([*coming, context], [], 1)
            pieces.append([right, left])

    sent = [along_group(outs[3 - d], 4 - d) for d in (1, 2, 3)]

    gain, bias = norm_gain.reshape(1, 768), norm_bias.reshape(1, 768)
    own_parts = [part for own in pieces for part in own]
    partial, kept = score(shard_index.reshape(1), own_parts, gallery_embed, context, [gain, bias])
    order = jnp.arange(32, dtype=jnp.int32)
    pick = image_of[None, :] == order[:, None]
    partial = partial.reshape(2, 32, 4)
    partial = jnp.sum(jnp.where(pick[:, None, :, None], partial[None], 0.0), axis=2)
    partial = lax.all_to_all(partial, "shard", split_axis=0, concat_axis=0, tiled=True)
    top = jnp.max(partial[:, 0], axis=0)
    normalizer = top + jnp.log(jnp.sum(partial[:, 1] * jnp.exp(partial[:, 0] - top[None]), axis=0))
    normalizer = hold([jnp.pad(normalizer.reshape(1, 4), ((0, 7), (0, 124)))], sent)[0]
    normalizer = lax.ppermute(normalizer, "group", [(h, g) for g, h in homes])[0, :4]

    layer_out = finish(x.reshape(1), [kept, *sent], output_weight, query_states, gain, bias)
    return (layer_out, normalizer)


def solution(mesh):
    placed = (
        P(("group", "shard"), None),
        P("shard", None),
        P("group", None),
        P(("group", "shard"), None, None),
        P("shard", None, None),
        P(("group", "shard"), None, None),
        P(),
        P(None, "group"),
        P(),
        P(),
        P(),
    )
    return jax.shard_map(
        on_device,
        mesh=mesh,
        in_specs=placed,
        out_specs=(P(("group", "shard"), None, None, None), P(("group", "shard"))),
        check_vma=False,
    )
```

```python
import functools
import math

import jax
import jax.numpy as jnp
from jax import lax
from jax.experimental import pallas as pl
from jax.experimental.pallas import tpu as pltpu
from jax.sharding import PartitionSpec as P

HEADS = 12
BLK = 256
HD = 64
NQ = 32
SLOTS = 12
TAIL = 3 * 128
BROWS = TAIL + 16
EXP_SCALE = math.log2(math.e) / math.sqrt(HD)
PARTS = ((64, 64), (128, 64), (192, 64))
IMAGE_AT, COUNT_AT, TABLE_AT = 1, 33, 65
F32 = jnp.float32
BF16 = jnp.bfloat16


def in_hbm(value):
    return pltpu.with_memory_space_constraint(value, pltpu.HBM)


def fetched(sources, targets, sems):
    copies = [
        pltpu.make_async_copy(source, target, sems.at[k])
        for k, (source, target) in enumerate(zip(sources, targets))
    ]
    for copy in copies:
        copy.start()
    for copy in copies:
        copy.wait()


def open_kernel(group_ref, *refs):
    block_ref, messages = refs[6], refs[7:11]
    patches_ref, weight_ref, caption_ref, probe_ref, states_ref, ask_ref, sems = refs[11:]
    fetched(refs[:6], refs[11:17], sems)
    across = (((1,), (1,)), ((), ()))
    patches = patches_ref[0]
    weight = weight_ref[...]
    last = lax.dot_general(patches[256:257], weight, across, preferred_element_type=F32)
    pad = jnp.zeros((1, HD), F32)
    captions = caption_ref[...].astype(F32)
    tail = [jnp.concatenate([last[:, h * HD : (h + 1) * HD], pad], axis=1) for h in range(3)]
    tail += [
        lax.shift_right_logical(probe_ref[...], 4).astype(F32),
        (probe_ref[...] & 15).astype(F32),
        jnp.zeros((3, 128), F32),
        captions[:, 0:128],
        captions[:, 128:256],
    ]
    block_ref[TAIL:BROWS, :] = jnp.concatenate(tail).astype(BF16)

    @pl.when(group_ref[0] < 4)
    def _():
        keys = lax.dot_general(patches[:256], weight, across, preferred_element_type=F32)
        for h in range(3):
            block_ref[h * 128 : (h + 1) * 128, 0:HD] = keys[:128, h * HD : (h + 1) * HD].astype(BF16)
            block_ref[h * 128 : (h + 1) * 128, HD:128] = keys[128:, h * HD : (h + 1) * HD].astype(BF16)

    @pl.when(group_ref[0] >= 4)
    def _():
        values = lax.dot_general(weight, patches[:256], across, preferred_element_type=F32)
        for h in range(3):
            rows = values[h * HD : (h + 1) * HD].astype(BF16)
            block_ref[h * 128 : h * 128 + HD] = rows[:, :128]
            block_ref[h * 128 + HD : (h + 1) * 128] = rows[:, 128:]

    queries = jnp.dot(states_ref[...].reshape(128, 768), ask_ref[...], preferred_element_type=F32)
    pad = jnp.zeros((128, HD), F32)
    x = lax.shift_right_logical(group_ref[0], 1)
    for k in range(4):
        rows = jnp.concatenate([queries[:, k * 192 : (k + 1) * 192], pad], axis=1).astype(BF16)
        for d in range(4):

            @pl.when(((k - x) & 3) == d)
            def _():
                messages[d][0:128, :] = rows


def opening(group, sources):
    vmem, hbm = pl.BlockSpec(memory_space=pltpu.VMEM), pl.BlockSpec(memory_space=pltpu.HBM)
    outs = pl.pallas_call(
        open_kernel,
        out_shape=[jax.ShapeDtypeStruct((BROWS, 128), BF16)]
        + [jax.ShapeDtypeStruct((144, 256), BF16)] * 4,
        in_specs=[pl.BlockSpec(memory_space=pltpu.SMEM)] + [hbm] * 6,
        out_specs=[vmem] * 5,
        scratch_shapes=[pltpu.VMEM(source.shape, source.dtype) for source in sources]
        + [pltpu.SemaphoreType.DMA((7,))],
        compiler_params=pltpu.CompilerParams(vmem_limit_bytes=12 * 1024 * 1024),
        name="opening",
    )(group, *[in_hbm(source) for source in sources])
    return outs[0], outs[1:]


def hold_kernel(*refs):
    pass


def hold(values, after, near=0):
    anywhere, vmem = pl.BlockSpec(memory_space=pl.ANY), pl.BlockSpec(memory_space=pltpu.VMEM)
    specs = [anywhere] * (len(values) - near) + [vmem] * near
    return pl.pallas_call(
        hold_kernel,
        out_shape=[jax.ShapeDtypeStruct(value.shape, value.dtype) for value in values],
        in_specs=specs + [anywhere] * len(after),
        out_specs=specs,
        input_output_aliases={k: k for k in range(len(values))},
        compiler_params=pltpu.CompilerParams(vmem_limit_bytes=1024 * 1024),
        name="hold",
    )(*values, *after)


def seal_kernel(*refs):
    candidate_ref, messages = refs[4], refs[-4:]
    ids = jnp.concatenate([candidate_ref[c] for c in range(4)], axis=1).astype(F32)
    tail = jnp.concatenate([ids, jnp.zeros((16, 252), F32)], axis=1).astype(BF16)
    for message in messages:
        message[128:144, :] = tail


def seal(messages, candidates, after):
    anywhere, vmem = pl.BlockSpec(memory_space=pl.ANY), pl.BlockSpec(memory_space=pltpu.VMEM)
    return pl.pallas_call(
        seal_kernel,
        out_shape=[jax.ShapeDtypeStruct((144, 256), BF16)] * 4,
        in_specs=[vmem] * 5 + [anywhere] * len(after),
        out_specs=[vmem] * 4,
        input_output_aliases={k: k for k in range(4)},
        compiler_params=pltpu.CompilerParams(vmem_limit_bytes=4 * 1024 * 1024),
        name="seal",
    )(*messages, candidates, *after)


def spread_kernel(q0, q1, q2, q3, query):
    left = lax.broadcasted_iota(jnp.int32, (128, 128), 1) < HD
    for d, q_ref in enumerate((q0, q1, q2, q3)):
        rows = q_ref[0:128, :].astype(F32)
        first, second = rows[:, 0:128], rows[:, 128:256]
        turned = pltpu.roll(first, HD, 1)
        parts = (
            (jnp.where(left, first, 0.0), jnp.where(left, 0.0, turned)),
            (jnp.where(left, turned, 0.0), jnp.where(left, 0.0, first)),
            (second, pltpu.roll(second, HD, 1)),
        )
        for h in range(3):
            for side in range(2):
                for c in range(4):
                    query[h, side, d * 4 + c] = parts[h][side][c * 32 : (c + 1) * 32].astype(BF16)


def spread(messages):
    vmem = pl.BlockSpec(memory_space=pltpu.VMEM)
    return pl.pallas_call(
        spread_kernel,
        out_shape=jax.ShapeDtypeStruct((3, 2, 16, NQ, 128), BF16),
        in_specs=[vmem] * 4,
        out_specs=vmem,
        compiler_params=pltpu.CompilerParams(vmem_limit_bytes=8 * 1024 * 1024),
        name="spread",
    )(*messages)


def attend_kernel(sizes, first_image, unroll, fresh, final, plan_ref, query_ref, *refs):
    parts = len(sizes)
    own_refs, other_refs = refs[:parts], refs[parts : 2 * parts]
    refs = refs[2 * parts + (0 if fresh else 1) :]
    context = refs[0]
    outs = refs[1:4] if final else ()
    query, held, column, tiles, sems = refs[1 + len(outs) :]
    images = sum(sizes)
    core = plan_ref[0]
    copies = [pltpu.make_async_copy(query_ref, query, sems.at[2 * parts])]
    start = 0
    for part, size in enumerate(sizes):
        for k, (source, kind) in enumerate(((own_refs[part], core), (other_refs[part], 1 - core))):
            target = held.at[kind, pl.ds(start, size)]
            copies.append(pltpu.make_async_copy(source, target, sems.at[2 * part + k]))
        start += size
    for copy in copies:
        copy.start()
    total = jnp.int32(0)
    for i in range(images):
        for t in range(3):
            tiles[total + t] = 4 * i + t
        amount = plan_ref[COUNT_AT + plan_ref[IMAGE_AT + first_image + i]]
        total = total + lax.shift_right_logical(amount + 3, 2)
    for copy in copies:
        copy.wait()
    for i in range(images):
        turned = held[1, i, TAIL:BROWS, :].astype(F32).T
        for h in range(3):
            column[i, h] = jnp.broadcast_to(turned[0:HD, h : h + 1], (HD, 128))

    def scores(code):
        i = lax.shift_right_logical(code, 2)
        image = plan_ref[IMAGE_AT + first_image + i]
        last = plan_ref[COUNT_AT + image] - 1
        first = (code & 3) * 4
        pairs = [plan_ref[TABLE_AT + image * SLOTS + jnp.minimum(first + j, last)] for j in range(4)]
        caps = [lax.shift_right_logical(p, 4) for p in pairs]
        found = []
        for h in range(3):
            q = jnp.concatenate(
                [query[h, 0, c] for c in caps] + [query[h, 1, c] for c in caps], axis=0
            )
            keys = jnp.concatenate([held[0, i, h * 128 : (h + 1) * 128, :], held[0, i, TAIL:BROWS, :]])
            found.append(
                lax.dot_general(
                    keys,
                    q,
                    (((1,), (1,)), ((), ())),
                    preferred_element_type=F32,
                )
            )
        return i, pairs, found

    def mix(i, pairs, found):
        contexts = []
        for h in range(3):
            s = found[h]
            top, bottom, cls = s[:128, :128], s[:128, 128:], s[128 + h : 129 + h, :128]
            highest = jnp.maximum(jnp.max(jnp.maximum(top, bottom), axis=0, keepdims=True), cls)
            e_top = jnp.exp2((top - highest) * EXP_SCALE)
            e_bottom = jnp.exp2((bottom - highest) * EXP_SCALE)
            e_cls = jnp.exp2((cls - highest) * EXP_SCALE)
            inverse = 1.0 / (jnp.sum(e_top + e_bottom, axis=0, keepdims=True) + e_cls)
            a_cls = (e_cls * inverse).astype(BF16).astype(F32)
            a = jnp.concatenate(
                [(e_top * inverse).astype(BF16), (e_bottom * inverse).astype(BF16)], axis=0
            )
            at = h * 128
            v = jnp.concatenate([held[1, i, at : at + HD, :], held[1, i, at + HD : at + 128, :]], axis=1)
            contexts.append(jnp.dot(v, a, preferred_element_type=F32) + column[i, h] * a_cls)
        both = jnp.concatenate(contexts[0:2], axis=0).astype(BF16).T
        third = jnp.concatenate([contexts[2], pltpu.roll(contexts[2], 128 - 16, 1)], axis=0)
        third = third.astype(BF16).T
        for j in range(4):
            context[pairs[j], 0:32, :] = both[j * 32 : (j + 1) * 32]
            context[pairs[j], 32:48, :] = third[j * 32 : j * 32 + 16]

    def group(g, carry):
        codes = [tiles[jnp.minimum(g * unroll + u, total - 1)] for u in range(unroll)]
        for item in [scores(code) for code in codes]:
            mix(*item)
        return carry

    lax.fori_loop(0, lax.div(total + unroll - 1, unroll), group, 0)
    if final:
        fetched([context.at[pl.ds(at, size)] for at, size in PARTS], outs, sems)


def attend(plan, first_image, query, own, other, context, final):
    sizes = tuple(part.shape[0] for part in own)
    images = sum(sizes)
    fresh = context is None
    vmem, anywhere = pl.BlockSpec(memory_space=pltpu.VMEM), pl.BlockSpec(memory_space=pl.ANY)
    pieces = [*own, *[in_hbm(part) for part in other]]
    operands = [in_hbm(plan), in_hbm(query), *pieces] + ([] if fresh else [context])
    parts = PARTS if final else ()
    outs = pl.pallas_call(
        functools.partial(attend_kernel, sizes, first_image, 5, fresh, final),
        out_shape=[jax.ShapeDtypeStruct((256, 48, 128), BF16)]
        + [jax.ShapeDtypeStruct((size, 48, 128), BF16) for _, size in parts],
        in_specs=[pl.BlockSpec(memory_space=pltpu.SMEM)]
        + [anywhere] * (1 + len(pieces))
        + ([] if fresh else [vmem]),
        out_specs=[vmem] + [pl.BlockSpec(memory_space=pltpu.HBM)] * len(parts),
        input_output_aliases={} if fresh else {len(operands) - 1: 0},
        scratch_shapes=[
            pltpu.VMEM(query.shape, BF16),
            pltpu.VMEM((2, images, BROWS, 128), BF16),
            pltpu.VMEM((images, 3, HD, 128), F32),
            pltpu.SMEM((images * 3 + 4,), jnp.int32),
            pltpu.SemaphoreType.DMA((7,)),
        ],
        cost_estimate=pl.CostEstimate(
            flops=images * 600_000_000, bytes_accessed=images * 800_000, transcendentals=images * 800_000
        ),
        compiler_params=pltpu.CompilerParams(vmem_limit_bytes=14 * 1024 * 1024),
        name="attend",
    )(*operands)
    return outs[0], outs[1:]


def score_kernel(shard_ref, *refs):
    count = len(refs) - 10
    pieces, gallery, context = refs[:count], refs[count], refs[count + 1]
    out_ref, kept, tails, rows, scores, sems = refs[count + 4 :]
    copies = [
        pltpu.make_async_copy(gallery, rows, sems.at[count]),
        pltpu.make_async_copy(context.at[pl.ds(0, 64)], kept, sems.at[count + 1]),
    ]
    start = 0
    for k, piece in enumerate(pieces):
        images = piece.shape[0]
        copies.append(
            pltpu.make_async_copy(
                piece.at[:, pl.ds(TAIL, 16), :], tails.at[pl.ds(start, images)], sems.at[k]
            )
        )
        start += images
    for copy in copies:
        copy.start()
    for copy in copies:
        copy.wait()
    scale = 1.0 / (0.07 * math.sqrt(256))
    first, second = [], []
    for i in range(32):
        tail = tails[i].astype(F32)
        first.append(tail[8:12])
        second.append(tail[12:16])
    captions = jnp.concatenate([jnp.concatenate(first), jnp.concatenate(second)], axis=1).astype(BF16)
    tail = tails[0].astype(F32)
    near = tail[3:4] == shard_ref[0].astype(F32)
    highest = jnp.full((8, 128), -1e30, F32)
    alive = []
    for b in range(16):
        hit = jnp.where(jnp.logical_and(near, tail[4:5] == float(b)), 1.0, 0.0)
        alive.append(jnp.broadcast_to(jnp.max(hit, axis=1, keepdims=True), (8, 128)) > 0.5)
        s = lax.dot_general(
            rows[b * BLK : (b + 1) * BLK], captions, (((1,), (1,)), ((), ())), preferred_element_type=F32
        )
        s = s * scale
        scores[b] = s
        most = jnp.max(s.reshape(BLK // 8, 8, 128), axis=0)
        highest = jnp.maximum(highest, jnp.where(alive[b], most, -1e30))
    top = jnp.max(highest, axis=0, keepdims=True)
    total = jnp.zeros((8, 128), F32)
    for b in range(16):
        e = jnp.sum(jnp.exp(scores[b] - top).reshape(BLK // 8, 8, 128), axis=0)
        total = total + jnp.where(alive[b], e, 0.0)
    out_ref[0:1, :] = top
    out_ref[1:2, :] = jnp.sum(total, axis=0, keepdims=True)


def score(shard, pieces, gallery, context, ready):
    hbm, vmem, anywhere = (pl.BlockSpec(memory_space=space) for space in (pltpu.HBM, pltpu.VMEM, pl.ANY))
    return pl.pallas_call(
        score_kernel,
        out_shape=[jax.ShapeDtypeStruct((2, 128), F32), jax.ShapeDtypeStruct((64, 48, 128), BF16)],
        in_specs=[pl.BlockSpec(memory_space=pltpu.SMEM)] + [anywhere] * (len(pieces) + 1) + [vmem] + [anywhere] * len(ready),
        out_specs=[vmem, hbm],
        scratch_shapes=[
            pltpu.VMEM((32, 16, 128), BF16),
            pltpu.VMEM(gallery.shape, BF16),
            pltpu.VMEM((16, BLK, 128), F32),
            pltpu.SemaphoreType.DMA((len(pieces) + 2,)),
        ],
        cost_estimate=pl.CostEstimate(flops=1000, bytes_accessed=1000, transcendentals=0),
        compiler_params=pltpu.CompilerParams(vmem_limit_bytes=12 * 1024 * 1024),
        name="score",
    )(shard, *pieces, gallery, context, *ready)


def finish_kernel(x_ref, c0, c1, c2, c3, weight_ref, states_ref, gain_ref, bias_ref, out_ref, main, third):
    @pl.when(pl.program_id(0) == 0)
    def _():
        for d in range(4):
            source = lax.rem(x_ref[0] + d, 4)
            main[d * 128 : (d + 1) * 128] = weight_ref[source, 0:128]
            third[d * 64 : (d + 1) * 64] = weight_ref[source, 128:192]

    parts = (c0, c1, c2, c3)
    count = c0.shape[0]
    first = jnp.concatenate([part[:, 0:32, :].reshape(count * 32, 128) for part in parts], axis=1)
    second = [part[:, 32:48, :].reshape(count * 16, 128) for part in parts]
    left = lax.broadcasted_iota(jnp.int32, second[0].shape, 1) < HD
    pairs = ((second[0], second[1]), (second[2], second[3]))
    lows = [jnp.where(left, one, jnp.concatenate([two[:, HD:], two[:, :HD]], axis=1)) for one, two in pairs]
    highs = [jnp.where(left, jnp.concatenate([one[:, HD:], one[:, :HD]], axis=1), two) for one, two in pairs]
    mixed = jnp.dot(first, main[...], preferred_element_type=F32).reshape(count, 2, 16, 768)
    early = jnp.dot(jnp.concatenate(lows, axis=1), third[...], preferred_element_type=F32).reshape(count, 16, 768)
    late = jnp.dot(jnp.concatenate(highs, axis=1), third[...], preferred_element_type=F32).reshape(count, 16, 768)
    states = states_ref[0].astype(F32)
    gain = gain_ref[...]
    bias = bias_ref[...]
    for half, extra in ((0, early), (1, late)):
        hidden = mixed[:, half] + extra + states[half * 16 : (half + 1) * 16][None]
        average = jnp.mean(hidden, axis=-1, keepdims=True)
        centered = hidden - average
        variance = jnp.mean(centered * centered, axis=-1, keepdims=True)
        out_ref[0, :, half * 16 : (half + 1) * 16, :] = (
            centered * lax.rsqrt(variance + 1e-06) * gain + bias
        ).astype(BF16)


def finish(x, contexts, output_weight, query_states, gain, bias):
    per_step = 16
    each = pl.BlockSpec((per_step, 48, 128), lambda s, *_: (s, 0, 0))
    return pl.pallas_call(
        finish_kernel,
        out_shape=jax.ShapeDtypeStruct((4, 16, NQ, 768), BF16),
        grid_spec=pltpu.PrefetchScalarGridSpec(
            num_scalar_prefetch=1,
            grid=(64 // per_step,),
            in_specs=[each] * 4
            + [
                pl.BlockSpec((4, 192, 768), lambda s, *_: (0, 0, 0)),
                pl.BlockSpec((1, NQ, 768), lambda s, *_: (s, 0, 0)),
                pl.BlockSpec((1, 768), lambda s, *_: (0, 0)),
                pl.BlockSpec((1, 768), lambda s, *_: (0, 0)),
            ],
            out_specs=pl.BlockSpec((1, 16, NQ, 768), lambda s, *_: (s, 0, 0, 0)),
            scratch_shapes=[pltpu.VMEM((512, 768), BF16), pltpu.VMEM((256, 768), BF16)],
        ),
        compiler_params=pltpu.CompilerParams(vmem_limit_bytes=32 * 1024 * 1024),
        name="finish",
    )(x, *[in_hbm(part) for part in (*contexts, output_weight.reshape(4, 192, 768), query_states, gain, bias)])


def grid_moves(dy, dz):
    return [
        (y * 8 + z, ((y + dy) % 4) * 8 + (z + dz) % 8) for y in range(4) for z in range(8)
    ]


def group_moves(dx, flip=0):
    return [(2 * x + c, 2 * ((x + dx) % 4) + (c ^ flip)) for x in range(4) for c in range(2)]


def on_device(
    caption_embed,
    gallery_embed,
    probe_blocks,
    query_states,
    patches,
    candidates,
    query_weight,
    keyvalue_weight,
    output_weight,
    norm_gain,
    norm_bias,
):
    group_index = lax.axis_index("group")
    shard_index = lax.axis_index("shard")
    x, core = group_index // 2, group_index % 2
    my_y, my_z = shard_index // 8, shard_index % 8
    cap_dev, tokens, model_width = query_states.shape

    def along_shard(value, dy, dz):
        return lax.ppermute(value, "shard", grid_moves(dy, dz))

    def along_group(value, dx, flip=0):
        return lax.ppermute(value, "group", group_moves(dx, flip))

    sources = [patches, keyvalue_weight.T, caption_embed, probe_blocks, query_states, query_weight]
    block, messages = opening(group_index.reshape(1), sources)
    homes = [(k, 2 * k) for k in range(4)] + [(4 + k, 2 * k + 1) for k in range(4)]

    def homeward(dy):
        moves = [(g * 32 + a, h * 32 + b) for g, h in homes for a, b in grid_moves(dy, 0)]
        return lax.ppermute(block, ("group", "shard"), moves)

    arrived = [homeward(dy) for dy in range(4)]
    messages = seal(messages, candidates, arrived[:2])
    received = [messages[0]] + [along_group(messages[4 - d], 4 - d) for d in (1, 2, 3)]
    stack = jnp.stack(arrived)
    pair_images = jnp.stack([part[128:144, :4].T for part in received]).reshape(256).astype(jnp.int32)
    numbers = jnp.arange(256, dtype=jnp.int32)
    same = pair_images[:, None] == pair_images[None, :]
    rank = jnp.sum(jnp.logical_and(same, numbers[None, :] < numbers[:, None]), axis=1)
    position = pair_images * SLOTS + rank
    places = jnp.arange(32 * SLOTS, dtype=jnp.int32)
    table = jnp.sum(
        jnp.where(position[None, :] == places[:, None], numbers[None, :], 0), axis=1
    ).astype(jnp.int32)
    count = jnp.sum(
        pair_images[None, :] == jnp.arange(32, dtype=jnp.int32)[:, None], axis=1
    ).astype(jnp.int32)

    query = spread(received)
    def images(y_shifts, z_shift):
        return [((my_y - dy) % 4) * 8 + (my_z - z_shift) % 8 for dy in y_shifts]

    whole = (0, 1, 2, 3)
    arrivals = images(whole, 0)
    for k in (1, 2, 3):
        arrivals += images(whole, k) + images(whole, -k)
    arrivals += images((0, 1), 4) + images((2, 3), -4)
    image_of = jnp.stack(arrivals).astype(jnp.int32)
    plan = jnp.concatenate([core.reshape(1).astype(jnp.int32), image_of, count, table, jnp.zeros((63,), jnp.int32)])

    pieces = [[stack]]
    waiting = []
    context, first_image = None, 0
    right = left = stack
    for step in range(5):
        if step < 3:
            coming = [along_shard(right, 0, 1), along_shard(left, 0, -1)]
        elif step == 3:
            coming = [along_shard(right[:2], 0, 1), along_shard(left[2:], 0, -1)]
        waiting += pieces[-1]
        if step > 0:
            if step == 1:
                waiting = [*hold([stack], received[1:]), *waiting[1:]]
            now, waiting = (waiting[:2], waiting[2:]) if step == 1 else (waiting, [])
            other = [along_group(part, 0, 1) for part in now]
            context, outs = attend(plan, first_image, query, now, other, context, step == 4)
            first_image += sum(part.shape[0] for part in now)
        if step < 4:
            right, left = coming
            if step > 0:
                right, left, context = hold([*coming, context], [], 1)
            pieces.append([right, left])

    sent = [along_group(outs[3 - d], 4 - d) for d in (1, 2, 3)]

    gain, bias = norm_gain.reshape(1, 768), norm_bias.reshape(1, 768)
    own_parts = [part for own in pieces for part in own]
    partial, kept = score(shard_index.reshape(1), own_parts, gallery_embed, context, [gain, bias])
    order = jnp.arange(32, dtype=jnp.int32)
    pick = image_of[None, :] == order[:, None]
    partial = partial.reshape(2, 32, 4)
    partial = jnp.sum(jnp.where(pick[:, None, :, None], partial[None], 0.0), axis=2)
    partial = lax.all_to_all(partial, "shard", split_axis=0, concat_axis=0, tiled=True)
    top = jnp.max(partial[:, 0], axis=0)
    normalizer = top + jnp.log(jnp.sum(partial[:, 1] * jnp.exp(partial[:, 0] - top[None]), axis=0))
    normalizer = hold([jnp.pad(normalizer.reshape(1, 4), ((0, 7), (0, 124)))], sent)[0]
    normalizer = lax.ppermute(normalizer, "group", [(h, g) for g, h in homes])[0, :4]

    layer_out = finish(x.reshape(1), [kept, *sent], output_weight, query_states, gain, bias)
    return (layer_out, normalizer)


def solution(mesh):
    placed = (
        P(("group", "shard"), None),
        P("shard", None),
        P("group", None),
        P(("group", "shard"), None, None),
        P("shard", None, None),
        P(("group", "shard"), None, None),
        P(),
        P(None, "group"),
        P(),
        P(),
        P(),
    )
    return jax.shard_map(
        on_device,
        mesh=mesh,
        in_specs=placed,
        out_specs=(P(("group", "shard"), None, None, None), P(("group", "shard"))),
        check_vma=False,
    )
```

```python
import functools
import math

import jax
import jax.numpy as jnp
from jax import lax
from jax.experimental import pallas as pl
from jax.experimental.pallas import tpu as pltpu
from jax.sharding import PartitionSpec as P

HEADS = 12
BLK = 256
HD = 64
NQ = 32
SLOTS = 12
TAIL = 3 * 128
BROWS = TAIL + 16
EXP_SCALE = math.log2(math.e) / math.sqrt(HD)
PARTS = ((64, 64), (128, 64), (192, 64))
IMAGE_AT, COUNT_AT, TABLE_AT = 1, 33, 65
F32 = jnp.float32
BF16 = jnp.bfloat16


def in_hbm(value):
    return pltpu.with_memory_space_constraint(value, pltpu.HBM)


def fetched(sources, targets, sems):
    copies = [
        pltpu.make_async_copy(source, target, sems.at[k])
        for k, (source, target) in enumerate(zip(sources, targets))
    ]
    for copy in copies:
        copy.start()
    for copy in copies:
        copy.wait()


def open_kernel(group_ref, *refs):
    block_ref, messages = refs[6], refs[7:11]
    patches_ref, weight_ref, caption_ref, probe_ref, states_ref, ask_ref, sems = refs[11:]
    fetched(refs[:6], refs[11:17], sems)
    across = (((1,), (1,)), ((), ()))
    patches = patches_ref[0]
    weight = weight_ref[...]
    last = lax.dot_general(patches[256:257], weight, across, preferred_element_type=F32)
    pad = jnp.zeros((1, HD), F32)
    captions = caption_ref[...].astype(F32)
    tail = [jnp.concatenate([last[:, h * HD : (h + 1) * HD], pad], axis=1) for h in range(3)]
    tail += [
        lax.shift_right_logical(probe_ref[...], 4).astype(F32),
        (probe_ref[...] & 15).astype(F32),
        jnp.zeros((3, 128), F32),
        captions[:, 0:128],
        captions[:, 128:256],
    ]
    block_ref[TAIL:BROWS, :] = jnp.concatenate(tail).astype(BF16)

    @pl.when(group_ref[0] < 4)
    def _():
        keys = lax.dot_general(patches[:256], weight, across, preferred_element_type=F32)
        for h in range(3):
            block_ref[h * 128 : (h + 1) * 128, 0:HD] = keys[:128, h * HD : (h + 1) * HD].astype(BF16)
            block_ref[h * 128 : (h + 1) * 128, HD:128] = keys[128:, h * HD : (h + 1) * HD].astype(BF16)

    @pl.when(group_ref[0] >= 4)
    def _():
        values = lax.dot_general(weight, patches[:256], across, preferred_element_type=F32)
        for h in range(3):
            rows = values[h * HD : (h + 1) * HD].astype(BF16)
            block_ref[h * 128 : h * 128 + HD] = rows[:, :128]
            block_ref[h * 128 + HD : (h + 1) * 128] = rows[:, 128:]

    queries = jnp.dot(states_ref[...].reshape(128, 768), ask_ref[...], preferred_element_type=F32)
    pad = jnp.zeros((128, HD), F32)
    x = lax.shift_right_logical(group_ref[0], 1)
    for k in range(4):
        rows = jnp.concatenate([queries[:, k * 192 : (k + 1) * 192], pad], axis=1).astype(BF16)
        for d in range(4):

            @pl.when(((k - x) & 3) == d)
            def _():
                messages[d][0:128, :] = rows


def opening(group, sources):
    vmem, hbm = pl.BlockSpec(memory_space=pltpu.VMEM), pl.BlockSpec(memory_space=pltpu.HBM)
    outs = pl.pallas_call(
        open_kernel,
        out_shape=[jax.ShapeDtypeStruct((BROWS, 128), BF16)]
        + [jax.ShapeDtypeStruct((144, 256), BF16)] * 4,
        in_specs=[pl.BlockSpec(memory_space=pltpu.SMEM)] + [hbm] * 6,
        out_specs=[vmem] * 5,
        scratch_shapes=[pltpu.VMEM(source.shape, source.dtype) for source in sources]
        + [pltpu.SemaphoreType.DMA((7,))],
        compiler_params=pltpu.CompilerParams(vmem_limit_bytes=12 * 1024 * 1024),
        name="opening",
    )(group, *[in_hbm(source) for source in sources])
    return outs[0], outs[1:]


def hold_kernel(*refs):
    pass


def hold(values, after, near=0):
    anywhere, vmem = pl.BlockSpec(memory_space=pl.ANY), pl.BlockSpec(memory_space=pltpu.VMEM)
    specs = [anywhere] * (len(values) - near) + [vmem] * near
    return pl.pallas_call(
        hold_kernel,
        out_shape=[jax.ShapeDtypeStruct(value.shape, value.dtype) for value in values],
        in_specs=specs + [anywhere] * len(after),
        out_specs=specs,
        input_output_aliases={k: k for k in range(len(values))},
        compiler_params=pltpu.CompilerParams(vmem_limit_bytes=1024 * 1024),
        name="hold",
    )(*values, *after)


def seal_kernel(*refs):
    candidate_ref, messages = refs[4], refs[-4:]
    ids = jnp.concatenate([candidate_ref[c] for c in range(4)], axis=1).astype(F32)
    tail = jnp.concatenate([ids, jnp.zeros((16, 252), F32)], axis=1).astype(BF16)
    for message in messages:
        message[128:144, :] = tail


def seal(messages, candidates, after):
    anywhere, vmem = pl.BlockSpec(memory_space=pl.ANY), pl.BlockSpec(memory_space=pltpu.VMEM)
    return pl.pallas_call(
        seal_kernel,
        out_shape=[jax.ShapeDtypeStruct((144, 256), BF16)] * 4,
        in_specs=[vmem] * 5 + [anywhere] * len(after),
        out_specs=[vmem] * 4,
        input_output_aliases={k: k for k in range(4)},
        compiler_params=pltpu.CompilerParams(vmem_limit_bytes=4 * 1024 * 1024),
        name="seal",
    )(*messages, candidates, *after)


def spread_kernel(q0, q1, q2, q3, query):
    left = lax.broadcasted_iota(jnp.int32, (128, 128), 1) < HD
    for d, q_ref in enumerate((q0, q1, q2, q3)):
        rows = q_ref[0:128, :].astype(F32)
        first, second = rows[:, 0:128], rows[:, 128:256]
        turned = pltpu.roll(first, HD, 1)
        parts = (
            (jnp.where(left, first, 0.0), jnp.where(left, 0.0, turned)),
            (jnp.where(left, turned, 0.0), jnp.where(left, 0.0, first)),
            (second, pltpu.roll(second, HD, 1)),
        )
        for h in range(3):
            for side in range(2):
                for c in range(4):
                    query[h, side, d * 4 + c] = parts[h][side][c * 32 : (c + 1) * 32].astype(BF16)


def spread(messages):
    vmem = pl.BlockSpec(memory_space=pltpu.VMEM)
    return pl.pallas_call(
        spread_kernel,
        out_shape=jax.ShapeDtypeStruct((3, 2, 16, NQ, 128), BF16),
        in_specs=[vmem] * 4,
        out_specs=vmem,
        compiler_params=pltpu.CompilerParams(vmem_limit_bytes=8 * 1024 * 1024),
        name="spread",
    )(*messages)


def attend_kernel(sizes, first_image, unroll, fresh, final, plan_ref, query_ref, *refs):
    parts = len(sizes)
    own_refs, other_refs = refs[:parts], refs[parts : 2 * parts]
    refs = refs[2 * parts + (0 if fresh else 1) :]
    context = refs[0]
    outs = refs[1:4] if final else ()
    query, held, column, tiles, sems = refs[1 + len(outs) :]
    images = sum(sizes)
    core = plan_ref[0]
    copies = [pltpu.make_async_copy(query_ref, query, sems.at[2 * parts])]
    start = 0
    for part, size in enumerate(sizes):
        for k, (source, kind) in enumerate(((own_refs[part], core), (other_refs[part], 1 - core))):
            target = held.at[kind, pl.ds(start, size)]
            copies.append(pltpu.make_async_copy(source, target, sems.at[2 * part + k]))
        start += size
    for copy in copies:
        copy.start()
    total = jnp.int32(0)
    for i in range(images):
        for t in range(3):
            tiles[total + t] = 4 * i + t
        amount = plan_ref[COUNT_AT + plan_ref[IMAGE_AT + first_image + i]]
        total = total + lax.shift_right_logical(amount + 3, 2)
    for copy in copies:
        copy.wait()
    for i in range(images):
        turned = held[1, i, TAIL:BROWS, :].astype(F32).T
        for h in range(3):
            column[i, h] = jnp.broadcast_to(turned[0:HD, h : h + 1], (HD, 128))

    def scores(code):
        i = lax.shift_right_logical(code, 2)
        image = plan_ref[IMAGE_AT + first_image + i]
        last = plan_ref[COUNT_AT + image] - 1
        first = (code & 3) * 4
        pairs = [plan_ref[TABLE_AT + image * SLOTS + jnp.minimum(first + j, last)] for j in range(4)]
        caps = [lax.shift_right_logical(p, 4) for p in pairs]
        found = []
        for h in range(3):
            q = jnp.concatenate(
                [query[h, 0, c] for c in caps] + [query[h, 1, c] for c in caps], axis=0
            )
            keys = jnp.concatenate([held[0, i, h * 128 : (h + 1) * 128, :], held[0, i, TAIL:BROWS, :]])
            found.append(
                lax.dot_general(
                    keys,
                    q,
                    (((1,), (1,)), ((), ())),
                    preferred_element_type=F32,
                )
            )
        return i, pairs, found

    def mix(i, pairs, found):
        contexts = []
        for h in range(3):
            s = found[h]
            top, bottom, cls = s[:128, :128], s[:128, 128:], s[128 + h : 129 + h, :128]
            highest = jnp.maximum(jnp.max(jnp.maximum(top, bottom), axis=0, keepdims=True), cls)
            e_top = jnp.exp2((top - highest) * EXP_SCALE)
            e_bottom = jnp.exp2((bottom - highest) * EXP_SCALE)
            e_cls = jnp.exp2((cls - highest) * EXP_SCALE)
            inverse = 1.0 / (jnp.sum(e_top + e_bottom, axis=0, keepdims=True) + e_cls)
            a_cls = (e_cls * inverse).astype(BF16).astype(F32)
            a = jnp.concatenate(
                [(e_top * inverse).astype(BF16), (e_bottom * inverse).astype(BF16)], axis=0
            )
            at = h * 128
            v = jnp.concatenate([held[1, i, at : at + HD, :], held[1, i, at + HD : at + 128, :]], axis=1)
            contexts.append(jnp.dot(v, a, preferred_element_type=F32) + column[i, h] * a_cls)
        both = jnp.concatenate(contexts[0:2], axis=0).astype(BF16).T
        third = jnp.concatenate([contexts[2], pltpu.roll(contexts[2], 128 - 16, 1)], axis=0)
        third = third.astype(BF16).T
        for j in range(4):
            context[pairs[j], 0:32, :] = both[j * 32 : (j + 1) * 32]
            context[pairs[j], 32:48, :] = third[j * 32 : j * 32 + 16]

    def group(g, carry):
        codes = [tiles[jnp.minimum(g * unroll + u, total - 1)] for u in range(unroll)]
        for item in [scores(code) for code in codes]:
            mix(*item)
        return carry

    lax.fori_loop(0, lax.div(total + unroll - 1, unroll), group, 0)
    if final:
        fetched([context.at[pl.ds(at, size)] for at, size in PARTS], outs, sems)


def attend(plan, first_image, query, own, other, context, final):
    sizes = tuple(part.shape[0] for part in own)
    images = sum(sizes)
    fresh = context is None
    vmem, anywhere = pl.BlockSpec(memory_space=pltpu.VMEM), pl.BlockSpec(memory_space=pl.ANY)
    pieces = [*own, *other]
    operands = [in_hbm(plan), in_hbm(query), *pieces] + ([] if fresh else [context])
    parts = PARTS if final else ()
    outs = pl.pallas_call(
        functools.partial(attend_kernel, sizes, first_image, 5, fresh, final),
        out_shape=[jax.ShapeDtypeStruct((256, 48, 128), BF16)]
        + [jax.ShapeDtypeStruct((size, 48, 128), BF16) for _, size in parts],
        in_specs=[pl.BlockSpec(memory_space=pltpu.SMEM)]
        + [anywhere] * (1 + len(pieces))
        + ([] if fresh else [vmem]),
        out_specs=[vmem] + [pl.BlockSpec(memory_space=pltpu.HBM)] * len(parts),
        input_output_aliases={} if fresh else {len(operands) - 1: 0},
        scratch_shapes=[
            pltpu.VMEM(query.shape, BF16),
            pltpu.VMEM((2, images, BROWS, 128), BF16),
            pltpu.VMEM((images, 3, HD, 128), F32),
            pltpu.SMEM((images * 3 + 4,), jnp.int32),
            pltpu.SemaphoreType.DMA((7,)),
        ],
        cost_estimate=pl.CostEstimate(
            flops=images * 600_000_000, bytes_accessed=images * 800_000, transcendentals=images * 800_000
        ),
        compiler_params=pltpu.CompilerParams(vmem_limit_bytes=14 * 1024 * 1024),
        name="attend",
    )(*operands)
    return outs[0], outs[1:]


def score_kernel(shard_ref, *refs):
    count = len(refs) - 10
    pieces, gallery, context = refs[:count], refs[count], refs[count + 1]
    out_ref, kept, tails, rows, scores, sems = refs[count + 4 :]
    copies = [
        pltpu.make_async_copy(gallery, rows, sems.at[count]),
        pltpu.make_async_copy(context.at[pl.ds(0, 64)], kept, sems.at[count + 1]),
    ]
    start = 0
    for k, piece in enumerate(pieces):
        images = piece.shape[0]
        copies.append(
            pltpu.make_async_copy(
                piece.at[:, pl.ds(TAIL, 16), :], tails.at[pl.ds(start, images)], sems.at[k]
            )
        )
        start += images
    for copy in copies:
        copy.start()
    for copy in copies:
        copy.wait()
    scale = 1.0 / (0.07 * math.sqrt(256))
    first, second = [], []
    for i in range(32):
        tail = tails[i].astype(F32)
        first.append(tail[8:12])
        second.append(tail[12:16])
    captions = jnp.concatenate([jnp.concatenate(first), jnp.concatenate(second)], axis=1).astype(BF16)
    tail = tails[0].astype(F32)
    near = tail[3:4] == shard_ref[0].astype(F32)
    highest = jnp.full((8, 128), -1e30, F32)
    alive = []
    for b in range(16):
        hit = jnp.where(jnp.logical_and(near, tail[4:5] == float(b)), 1.0, 0.0)
        alive.append(jnp.broadcast_to(jnp.max(hit, axis=1, keepdims=True), (8, 128)) > 0.5)
        s = lax.dot_general(
            rows[b * BLK : (b + 1) * BLK], captions, (((1,), (1,)), ((), ())), preferred_element_type=F32
        )
        s = s * scale
        scores[b] = s
        most = jnp.max(s.reshape(BLK // 8, 8, 128), axis=0)
        highest = jnp.maximum(highest, jnp.where(alive[b], most, -1e30))
    top = jnp.max(highest, axis=0, keepdims=True)
    total = jnp.zeros((8, 128), F32)
    for b in range(16):
        e = jnp.sum(jnp.exp(scores[b] - top).reshape(BLK // 8, 8, 128), axis=0)
        total = total + jnp.where(alive[b], e, 0.0)
    out_ref[0:1, :] = top
    out_ref[1:2, :] = jnp.sum(total, axis=0, keepdims=True)


def score(shard, pieces, gallery, context, ready):
    hbm, vmem, anywhere = (pl.BlockSpec(memory_space=space) for space in (pltpu.HBM, pltpu.VMEM, pl.ANY))
    return pl.pallas_call(
        score_kernel,
        out_shape=[jax.ShapeDtypeStruct((2, 128), F32), jax.ShapeDtypeStruct((64, 48, 128), BF16)],
        in_specs=[pl.BlockSpec(memory_space=pltpu.SMEM)] + [anywhere] * (len(pieces) + 1) + [vmem] + [anywhere] * len(ready),
        out_specs=[vmem, hbm],
        scratch_shapes=[
            pltpu.VMEM((32, 16, 128), BF16),
            pltpu.VMEM(gallery.shape, BF16),
            pltpu.VMEM((16, BLK, 128), F32),
            pltpu.SemaphoreType.DMA((len(pieces) + 2,)),
        ],
        cost_estimate=pl.CostEstimate(flops=1000, bytes_accessed=1000, transcendentals=0),
        compiler_params=pltpu.CompilerParams(vmem_limit_bytes=12 * 1024 * 1024),
        name="score",
    )(shard, *pieces, gallery, context, *ready)


def finish_kernel(x_ref, c0, c1, c2, c3, weight_ref, states_ref, gain_ref, bias_ref, out_ref, main, third):
    @pl.when(pl.program_id(0) == 0)
    def _():
        for d in range(4):
            source = lax.rem(x_ref[0] + d, 4)
            main[d * 128 : (d + 1) * 128] = weight_ref[source, 0:128]
            third[d * 64 : (d + 1) * 64] = weight_ref[source, 128:192]

    parts = (c0, c1, c2, c3)
    count = c0.shape[0]
    first = jnp.concatenate([part[:, 0:32, :].reshape(count * 32, 128) for part in parts], axis=1)
    second = [part[:, 32:48, :].reshape(count * 16, 128) for part in parts]
    left = lax.broadcasted_iota(jnp.int32, second[0].shape, 1) < HD
    pairs = ((second[0], second[1]), (second[2], second[3]))
    lows = [jnp.where(left, one, jnp.concatenate([two[:, HD:], two[:, :HD]], axis=1)) for one, two in pairs]
    highs = [jnp.where(left, jnp.concatenate([one[:, HD:], one[:, :HD]], axis=1), two) for one, two in pairs]
    mixed = jnp.dot(first, main[...], preferred_element_type=F32).reshape(count, 2, 16, 768)
    early = jnp.dot(jnp.concatenate(lows, axis=1), third[...], preferred_element_type=F32).reshape(count, 16, 768)
    late = jnp.dot(jnp.concatenate(highs, axis=1), third[...], preferred_element_type=F32).reshape(count, 16, 768)
    states = states_ref[0].astype(F32)
    gain = gain_ref[...]
    bias = bias_ref[...]
    for half, extra in ((0, early), (1, late)):
        hidden = mixed[:, half] + extra + states[half * 16 : (half + 1) * 16][None]
        average = jnp.mean(hidden, axis=-1, keepdims=True)
        centered = hidden - average
        variance = jnp.mean(centered * centered, axis=-1, keepdims=True)
        out_ref[0, :, half * 16 : (half + 1) * 16, :] = (
            centered * lax.rsqrt(variance + 1e-06) * gain + bias
        ).astype(BF16)


def finish(x, contexts, output_weight, query_states, gain, bias):
    per_step = 16
    each = pl.BlockSpec((per_step, 48, 128), lambda s, *_: (s, 0, 0))
    return pl.pallas_call(
        finish_kernel,
        out_shape=jax.ShapeDtypeStruct((4, 16, NQ, 768), BF16),
        grid_spec=pltpu.PrefetchScalarGridSpec(
            num_scalar_prefetch=1,
            grid=(64 // per_step,),
            in_specs=[each] * 4
            + [
                pl.BlockSpec((4, 192, 768), lambda s, *_: (0, 0, 0)),
                pl.BlockSpec((1, NQ, 768), lambda s, *_: (s, 0, 0)),
                pl.BlockSpec((1, 768), lambda s, *_: (0, 0)),
                pl.BlockSpec((1, 768), lambda s, *_: (0, 0)),
            ],
            out_specs=pl.BlockSpec((1, 16, NQ, 768), lambda s, *_: (s, 0, 0, 0)),
            scratch_shapes=[pltpu.VMEM((512, 768), BF16), pltpu.VMEM((256, 768), BF16)],
        ),
        compiler_params=pltpu.CompilerParams(vmem_limit_bytes=32 * 1024 * 1024),
        name="finish",
    )(x, *[in_hbm(part) for part in (*contexts, output_weight.reshape(4, 192, 768), query_states, gain, bias)])


def grid_moves(dy, dz):
    return [
        (y * 8 + z, ((y + dy) % 4) * 8 + (z + dz) % 8) for y in range(4) for z in range(8)
    ]


def group_moves(dx, flip=0):
    return [(2 * x + c, 2 * ((x + dx) % 4) + (c ^ flip)) for x in range(4) for c in range(2)]


def on_device(
    caption_embed,
    gallery_embed,
    probe_blocks,
    query_states,
    patches,
    candidates,
    query_weight,
    keyvalue_weight,
    output_weight,
    norm_gain,
    norm_bias,
):
    group_index = lax.axis_index("group")
    shard_index = lax.axis_index("shard")
    x, core = group_index // 2, group_index % 2
    my_y, my_z = shard_index // 8, shard_index % 8
    cap_dev, tokens, model_width = query_states.shape

    def along_shard(value, dy, dz):
        return lax.ppermute(value, "shard", grid_moves(dy, dz))

    def along_group(value, dx, flip=0):
        return lax.ppermute(value, "group", group_moves(dx, flip))

    sources = [patches, keyvalue_weight.T, caption_embed, probe_blocks, query_states, query_weight]
    block, messages = opening(group_index.reshape(1), sources)
    homes = [(k, 2 * k) for k in range(4)] + [(4 + k, 2 * k + 1) for k in range(4)]

    def homeward(dy):
        moves = [(g * 32 + a, h * 32 + b) for g, h in homes for a, b in grid_moves(dy, 0)]
        return lax.ppermute(block, ("group", "shard"), moves)

    arrived = [homeward(dy) for dy in range(4)]
    messages = seal(messages, candidates, arrived[:2])
    received = [messages[0]] + [along_group(messages[4 - d], 4 - d) for d in (1, 2, 3)]
    stack = jnp.stack(arrived)
    pair_images = jnp.stack([part[128:144, :4].T for part in received]).reshape(256).astype(jnp.int32)
    numbers = jnp.arange(256, dtype=jnp.int32)
    same = pair_images[:, None] == pair_images[None, :]
    rank = jnp.sum(jnp.logical_and(same, numbers[None, :] < numbers[:, None]), axis=1)
    position = pair_images * SLOTS + rank
    places = jnp.arange(32 * SLOTS, dtype=jnp.int32)
    table = jnp.sum(
        jnp.where(position[None, :] == places[:, None], numbers[None, :], 0), axis=1
    ).astype(jnp.int32)
    count = jnp.sum(
        pair_images[None, :] == jnp.arange(32, dtype=jnp.int32)[:, None], axis=1
    ).astype(jnp.int32)

    query = spread(received)
    def images(y_shifts, z_shift):
        return [((my_y - dy) % 4) * 8 + (my_z - z_shift) % 8 for dy in y_shifts]

    whole = (0, 1, 2, 3)
    arrivals = images(whole, 0)
    for k in (1, 2, 3):
        arrivals += images(whole, k) + images(whole, -k)
    arrivals += images((0, 1), 4) + images((2, 3), -4)
    image_of = jnp.stack(arrivals).astype(jnp.int32)
    plan = jnp.concatenate([core.reshape(1).astype(jnp.int32), image_of, count, table, jnp.zeros((63,), jnp.int32)])

    pieces = [[stack]]
    waiting = []
    context, first_image = None, 0
    right = left = stack
    for step in range(5):
        if step < 3:
            coming = [along_shard(right, 0, 1), along_shard(left, 0, -1)]
        elif step == 3:
            coming = [along_shard(right[:2], 0, 1), along_shard(left[2:], 0, -1)]
        waiting += pieces[-1]
        if step > 0:
            if step == 1:
                waiting = [*hold([stack], received[1:]), *waiting[1:]]
            now, waiting = (waiting[:2], waiting[2:]) if step == 1 else (waiting, [])
            other = [along_group(part, 0, 1) for part in now]
            if step not in (2, 3):
                other = [in_hbm(part) for part in other]
            context, outs = attend(plan, first_image, query, now, other, context, step == 4)
            first_image += sum(part.shape[0] for part in now)
        if step < 4:
            right, left = coming
            if step > 0:
                right, left, context = hold([*coming, context], [], 1)
            pieces.append([right, left])

    sent = [along_group(outs[3 - d], 4 - d) for d in (1, 2, 3)]

    gain, bias = norm_gain.reshape(1, 768), norm_bias.reshape(1, 768)
    own_parts = [part for own in pieces for part in own]
    partial, kept = score(shard_index.reshape(1), own_parts, gallery_embed, context, [gain, bias])
    order = jnp.arange(32, dtype=jnp.int32)
    pick = image_of[None, :] == order[:, None]
    partial = partial.reshape(2, 32, 4)
    partial = jnp.sum(jnp.where(pick[:, None, :, None], partial[None], 0.0), axis=2)
    partial = lax.all_to_all(partial, "shard", split_axis=0, concat_axis=0, tiled=True)
    top = jnp.max(partial[:, 0], axis=0)
    normalizer = top + jnp.log(jnp.sum(partial[:, 1] * jnp.exp(partial[:, 0] - top[None]), axis=0))
    normalizer = hold([jnp.pad(normalizer.reshape(1, 4), ((0, 7), (0, 124)))], sent)[0]
    normalizer = lax.ppermute(normalizer, "group", [(h, g) for g, h in homes])[0, :4]

    layer_out = finish(x.reshape(1), [kept, *sent], output_weight, query_states, gain, bias)
    return (layer_out, normalizer)


def solution(mesh):
    placed = (
        P(("group", "shard"), None),
        P("shard", None),
        P("group", None),
        P(("group", "shard"), None, None),
        P("shard", None, None),
        P(("group", "shard"), None, None),
        P(),
        P(None, "group"),
        P(),
        P(),
        P(),
    )
    return jax.shard_map(
        on_device,
        mesh=mesh,
        in_specs=placed,
        out_specs=(P(("group", "shard"), None, None, None), P(("group", "shard"))),
        check_vma=False,
    )
```
